32 devices in a mesh: grp: 1, dev: 16 (over z, y, core), section: 2 (over x), tp: 1.
Axes of the slice: x: 2, y: 2, z: 4, core: 2. Of those that a mesh axis runs over, the one named last changes fastest.
Arguments:
- prompt_pages: bfloat16 [32, 32, 16, 576], P(('grp', 'dev', 'section', 'tp')), may hold values from -6 to 6
- send_page: int32 [32, 32], P(('grp', 'dev', 'section', 'tp')), may hold values from -1 to 31, as said below
- page_table: int32 [32, 2, 16], P(('grp', 'dev', 'section', 'tp')), may hold values from -1 to 31, as said below
- context_len: int32 [32, 2], P(('grp', 'dev', 'section', 'tp')), may hold values from 1 to 256, as said below
- new_latent: bfloat16 [32, 2, 4, 576], P(('grp', 'dev', 'section', 'tp')), may hold values from -8 to 8
- queries: bfloat16 [32, 2, 4, 64, 576], P(('grp', 'dev', 'section', 'tp')), may hold values from -120 to 120
- moe_rows: bfloat16 [32, 4, 3584], P(('grp', 'dev', 'section', 'tp')), may hold values from -6 to 6
- routing: int32 [32, 4, 8], P(('grp', 'dev', 'section', 'tp')), may hold values from 0 to 15, all different within a row; in each aligned block of 4 rows (0 to 3, 4 to 7, ..., all dimensions but the last counted through in order) at most 3 rows name the same one
- gate_weights: float32 [32, 4, 8], P(('grp', 'dev', 'section', 'tp')), may hold values from 0.05 to 0.5
- expert_gate: bfloat16 [16, 3584, 1024], P('dev', None, ('section', 'tp')), may hold values from -0.09375 to 0.09375
- expert_up: bfloat16 [16, 3584, 1024], P('dev', None, ('section', 'tp')), may hold values from -0.09375 to 0.09375
- expert_down: bfloat16 [16, 1024, 3584], P('dev', ('section', 'tp')), may hold values from -0.1875 to 0.1875
Outputs:
- attended: bfloat16 [32, 2, 4, 64, 512], P(('grp', 'dev', 'section', 'tp'))
- expert_out: bfloat16 [32, 4, 3584], P(('grp', 'dev', 'section', 'tp'))
The draws below stay inside these ranges and needn't reach their ends.
Inputs may be any that keep to these rules, and one draw needn't show every extreme that they name: context_len of some request of every rank is exactly 256. `page_table`: of a rank's entries, those with p < ceil(context_len / 16) are distinct slots, all others -1. `send_page`: an outgoing slot holds a page exactly when the receiving rank's page_table names it; the pages of one rank named are distinct. `routing`: no rank names one expert in more than 3 of its assignments.
All inputs are finite; a program needn't handle non-finite values.
Results may differ from the reference program's by a relative error of at most 0.02.
Values may be sent and summed in bfloat16 or wider, within the bound.
No kernel may reach another device: no remote copies, remote signals or barrier semaphores. Data moves between devices by JAX's collectives and lax.ppermute only.
A program may use at most 64 MiB of HBM per device.

```python
import math
import jax
import jax.numpy as jnp
import numpy as np
from jax import lax

D = 3584
EHID = 1024
HEADS = 64
VDIM = 512
TOPK = 8
STEPS = 4
REQ = 2
PAGE = 16
CAPP = 2
ROWS = 4
LAT = 576
DEVS = 32
HBLOCKS = 2
EXPERTS = 16
CAPE = 3
SLOTS = 32
PAGES_DEV = 32
MAXP = 16
CTX = 256
N_DEV = 16


def layout(key):
    groups = DEVS // N_DEV
    key_len = jax.random.fold_in(key, 101)
    key_star = jax.random.fold_in(key, 102)
    key_perm = jax.random.fold_in(key, 103)
    key_local = jax.random.fold_in(key, 104)
    lengths = jax.random.randint(key_len, (DEVS, REQ), 1, CTX + 1)
    star = jax.random.randint(key_star, (DEVS, 1), 0, REQ)
    lengths = jnp.where(jnp.arange(REQ)[None, :] == star, CTX, lengths).astype(jnp.int32)
    pages_used = (lengths + PAGE - 1) // PAGE
    order = jax.vmap(lambda k: jax.random.permutation(k, SLOTS))(jax.random.split(key_perm, DEVS)).astype(jnp.int32)
    index = jnp.arange(SLOTS)
    used_q = index[None, :] % MAXP < pages_used[:, index // MAXP]
    table = jnp.where(used_q, order, -1).reshape(DEVS, REQ, MAXP).astype(jnp.int32)
    inverse = jnp.argsort(order, axis=1)
    used_recv = jnp.take_along_axis(used_q, inverse, axis=1)
    used_send = used_recv.reshape(N_DEV, groups, N_DEV, CAPP).transpose(2, 1, 0, 3).reshape(DEVS, SLOTS)
    local = jax.vmap(lambda k: jax.random.permutation(k, PAGES_DEV))(jax.random.split(key_local, DEVS)).astype(jnp.int32)
    send = jnp.where(used_send, local[:, :SLOTS], -1).astype(jnp.int32)
    return (lengths, table, send)


def latent_base(key):
    base = jax.random.normal(jax.random.fold_in(key, 201), (DEVS, REQ, STEPS, LAT), jnp.float32)
    return jnp.clip(base, -8.0, 8.0)


def draw_send_page(key, part):
    return layout(key)[2]


def draw_page_table(key, part):
    return layout(key)[1]


def draw_context_len(key, part):
    return layout(key)[0]


def draw_new_latent(key, part):
    return latent_base(key).astype(jnp.bfloat16)


def draw_queries(key, part):
    key = jax.random.fold_in(key, 7)
    key_noise = jax.random.fold_in(key, 2)
    values = jnp.clip(jax.random.normal(key_noise, (DEVS, REQ, STEPS, HEADS, LAT), jnp.float32), -6.0, 6.0)
    return values.astype(jnp.bfloat16)


def block_scale(stream_key, extent, pieces, smallest, high):
    def one(axis_at, blocks):
        steps = jax.random.uniform(jax.random.fold_in(jax.random.fold_in(stream_key, 6), axis_at), (blocks,), jnp.float32, smallest / len(pieces), high / len(pieces))
        return jnp.repeat(jnp.exp(steps), extent[axis_at] // blocks).reshape((-1,) + (1,) * (len(extent) - axis_at - 1))

    gain = one(*pieces[0])
    for cut in pieces[1:]:
        gain = gain * one(*cut)
    return gain


def assign_block(own_key, own, number, rows, number_of, top, limit, lean):
    sequence = jax.random.permutation(own_key, number_of)
    crowded, ordinary = load_shares(number_of, rows * top, limit, lean, True), load_shares(number_of, rows * top, limit, lean, False)
    places = jnp.arange(number_of)

    def named(sizes, turn):
        used = int((sizes > 0).sum())
        fixed = max(1, used // 4)
        passed = fixed + (places - fixed + turn * (used - fixed)) % max(1, number_of - fixed)
        return jnp.zeros((number_of,), jnp.int32).at[sequence[jnp.where(places < fixed, places, passed)]].set(jnp.asarray(sizes, jnp.int32))

    sizes = jnp.where(number % 4 == 0, named(crowded, number // 4), named(ordinary, number - number // 4 - 1))
    mixed = jax.random.permutation(jax.random.fold_in(own, 3), number_of)
    giver, taker = mixed[0:number_of // 2 * 2:2], mixed[1:number_of // 2 * 2:2]
    room = jnp.minimum(sizes[giver] - 1, limit - sizes[taker]) // 2
    room = jnp.where((giver == sequence[0]) | (taker == sequence[0]) | (sizes[taker] == 0), 0, jnp.maximum(room, 0))
    passed = jax.random.randint(jax.random.fold_in(own, 4), (number_of // 2,), 0, 1 << 20) % (room + 1)
    sizes = sizes.at[giver].add(-passed).at[taker].add(passed)
    labels = jnp.searchsorted(jnp.cumsum(sizes), jnp.arange(rows * top), side="right").astype(jnp.int32)
    listing = labels.reshape(top, rows).T
    listing = listing[jax.random.permutation(jax.random.fold_in(own, 1), rows)]
    turn = jax.random.randint(jax.random.fold_in(own, 2), (rows, 1), 0, top)
    return jnp.take_along_axis(listing, (jnp.arange(top)[None, :] + turn) % top, axis=1)


def load_shares(number_of, total, limit, slope, full):
    portions = [(1 << 20) // math.isqrt(rank ** slope) + 1 for rank in range(1, number_of + 1)]
    largest = limit if full else min(limit, max(-(-total // number_of), total * portions[0] // sum(portions)))
    least = 1 if total - largest >= number_of - 1 else 0
    given, rest = [largest] + [least] * (number_of - 1), total - largest - least * (number_of - 1)
    while rest > 0:
        movable = [i for i in range(1, number_of) if given[i] < largest] or [i for i in range(1, number_of) if given[i] < limit]
        pool, left = sum([portions[i] for i in movable]), rest
        for i in movable:
            addition = min(limit - given[i], max(1, left * portions[i] // pool), rest)
            given[i] = given[i] + addition
            rest = rest - addition
    return np.array(given)


def bell_draw(own_key, dims, deviation, most, cuts=(), kind=jnp.bfloat16):
    gain = block_scale(own_key, dims, cuts, -0.22, 0.18) if cuts else 1.0
    array = jax.random.normal(own_key, dims, jnp.float32) * deviation * gain
    return jnp.minimum(jnp.maximum(array, -most), most).astype(kind)


def setup_inputs(seed: int = 0, part: int = 0) -> dict:
    seeds = jax.random.split(jax.random.key(seed), 13)
    part_keys = jax.random.split(jax.random.fold_in(seeds[12], part), 13)
    prompt_pages = bell_draw(part_keys[0], (DEVS, PAGES_DEV, PAGE, LAT), 1.0, 6.0, ((0, 32),))
    send_page = draw_send_page(jax.random.fold_in(jax.random.fold_in(seeds[12], part), 71), part)
    page_table = draw_page_table(jax.random.fold_in(jax.random.fold_in(seeds[12], part), 71), part)
    context_len = draw_context_len(jax.random.fold_in(jax.random.fold_in(seeds[12], part), 71), part)
    new_latent = draw_new_latent(jax.random.fold_in(jax.random.fold_in(seeds[12], part), 71), part)
    queries = draw_queries(jax.random.fold_in(jax.random.fold_in(seeds[12], part), 71), part)
    moe_rows = bell_draw(part_keys[6], (DEVS, ROWS, D), 1.0, 6.0, ((0, 32),))
    routing_keys = jax.random.split(jax.random.fold_in(part_keys[7], 1), DEVS * ROWS // ROWS)
    routing_turns = jax.random.permutation(jax.random.fold_in(part_keys[7], 3), DEVS * ROWS // ROWS)
    routing = jax.vmap(lambda own, number: assign_block(jax.random.fold_in(part_keys[7], 2), own, number, ROWS, EXPERTS, TOPK, CAPE, 2))(routing_keys, routing_turns).reshape((DEVS, ROWS, TOPK))
    gate_weights = jnp.clip(jnp.exp(math.log(0.5) - 2.3025851 * jax.random.uniform(part_keys[8], (DEVS, ROWS, TOPK), jnp.float32) ** block_scale(part_keys[8], (DEVS, ROWS, TOPK), ((0, 32),), -0.2, 0.2)), 0.05, 0.5)
    expert_gate = bell_draw(seeds[9], (EXPERTS, D, EHID), D ** -0.5, 0.09375, ((0, 16), (2, 2)))
    expert_up = bell_draw(seeds[10], (EXPERTS, D, EHID), D ** -0.5, 0.09375, ((0, 16), (2, 2)))
    expert_down = bell_draw(seeds[11], (EXPERTS, EHID, D), EHID ** -0.5, 0.1875, ((0, 16), (1, 2)))
    return {"prompt_pages": prompt_pages, "send_page": send_page, "page_table": page_table, "context_len": context_len, "new_latent": new_latent, "queries": queries, "moe_rows": moe_rows, "routing": routing, "gate_weights": gate_weights, "expert_gate": expert_gate, "expert_up": expert_up, "expert_down": expert_down}


SCALE = 192.0 ** -0.5


def attend_one(queries, new_latent, cache, lengths):
    keys = jnp.concatenate([cache, new_latent], axis=1)
    scores = jnp.einsum("rshl,rkl->rshk", queries.astype(jnp.float32), keys.astype(jnp.float32)) * SCALE
    position = jnp.arange(CTX + STEPS)
    step_index = jnp.arange(STEPS)
    in_cache = position[None, :] < lengths[:, None]
    in_new = (position[None, :] >= CTX) & (position[None, :] - CTX <= step_index[:, None])
    allowed = in_cache[:, None, :] | in_new[None, :, :]
    scores = jnp.where(allowed[:, :, None, :], scores, -jnp.inf)
    top = jnp.max(scores, axis=-1, keepdims=True)
    weights = jnp.exp(scores - top)
    weights = (weights / jnp.sum(weights, axis=-1, keepdims=True)).astype(jnp.bfloat16)
    values = keys[:, :, :VDIM]
    return jnp.einsum("rshk,rkv->rshv", weights.astype(jnp.float32), values.astype(jnp.float32)).astype(jnp.bfloat16)


def expert_ffn(rows, w_gate, w_up, w_down):
    gate = jnp.dot(rows, w_gate, preferred_element_type=jnp.float32)
    up = jnp.dot(rows, w_up, preferred_element_type=jnp.float32)
    hidden = (jax.nn.silu(gate) * up).astype(jnp.bfloat16)
    count = hidden.shape[0]
    blocked = hidden.reshape(count, HBLOCKS, EHID // HBLOCKS).astype(jnp.float32)
    down_blocks = w_down.reshape(HBLOCKS, EHID // HBLOCKS, D).astype(jnp.float32)
    partial_value = jnp.einsum("rbh,bhd->brd", blocked, down_blocks).astype(jnp.bfloat16)
    return jnp.sum(partial_value.astype(jnp.float32), axis=0).astype(jnp.bfloat16)


def reference(prompt_pages, send_page, page_table, context_len, new_latent, queries, moe_rows, routing, gate_weights, expert_gate, expert_up, expert_down):
    groups = DEVS // N_DEV
    rank = jnp.arange(DEVS).astype(jnp.int32)
    dev_of = (rank // groups)[:, None, None]
    group_of = (rank % groups)[:, None, None]
    safe = jnp.maximum(page_table, 0)
    source = (safe // CAPP) * groups + group_of
    local = send_page[source, dev_of * CAPP + safe % CAPP]
    local = jnp.maximum(local, 0)
    cache = prompt_pages[source, local].reshape(DEVS, REQ, CTX, LAT)

    def attend_rank(items):
        return attend_one(items[0], items[1], items[2], items[3])

    attended = lax.map(attend_rank, (queries, new_latent, cache, context_len))

    ids = routing.reshape(DEVS, ROWS * TOPK)
    onehot = (ids[:, :, None] == jnp.arange(EXPERTS)[None, None, :]).astype(jnp.int32)
    earlier = jnp.cumsum(onehot, axis=1) - onehot
    slot = jnp.sum(earlier * onehot, axis=2).astype(jnp.int32)
    source_rank = jnp.broadcast_to(rank[:, None], ids.shape)
    row_of = (rank[:, None] * ROWS + jnp.arange(ROWS * TOPK)[None, :] // TOPK).astype(jnp.int32)
    table = jnp.full((EXPERTS, DEVS, CAPE), -1, jnp.int32).at[ids, source_rank, slot].set(row_of)
    weight_table = jnp.zeros((EXPERTS, DEVS, CAPE), jnp.float32).at[ids, source_rank, slot].set(gate_weights.reshape(DEVS, ROWS * TOPK))
    flat_rows = moe_rows.reshape(DEVS * ROWS, D)

    def one_expert(total, items):
        rows_index, weights, w_gate, w_up, w_down = items
        safe_rows = jnp.maximum(rows_index, 0).reshape(-1)
        answer = expert_ffn(flat_rows[safe_rows], w_gate, w_up, w_down)
        term = answer.astype(jnp.float32) * weights.reshape(-1)[:, None]
        return total.at[safe_rows].add(term), None

    total, _ = lax.scan(one_expert, jnp.zeros((DEVS * ROWS, D), jnp.float32), (table, weight_table, expert_gate, expert_up, expert_down))
    expert_out = total.reshape(DEVS, ROWS, D).astype(jnp.bfloat16)
    return attended, expert_out
```

```python
import jax
import jax.numpy as jnp
from jax import lax
from jax.sharding import PartitionSpec as P

VDIM = 512
SCALE = 192.0 ** (-0.5)
RANK = ("dev", "section", "tp")


def attend(queries, new_latent, cache, lengths):
    steps = queries.shape[1]
    ctx = cache.shape[1]
    keys = jnp.concatenate([cache, new_latent], axis=1)
    scores = jnp.einsum("rshl,rkl->rshk", queries, keys, preferred_element_type=jnp.float32) * SCALE
    position = jnp.arange(ctx + steps)
    step_index = jnp.arange(steps)
    in_cache = position[None, :] < lengths[:, None]
    in_new = (position[None, :] >= ctx) & (position[None, :] - ctx <= step_index[:, None])
    allowed = in_cache[:, None, :] | in_new[None, :, :]
    scores = jnp.where(allowed[:, :, None, :], scores, -jnp.inf)
    top = jnp.max(scores, axis=-1, keepdims=True)
    weights = jnp.exp(scores - top)
    weights = (weights / jnp.sum(weights, axis=-1, keepdims=True)).astype(jnp.bfloat16)
    values = keys[:, :, :VDIM]
    return jnp.einsum("rshk,rkv->rshv", weights, values, preferred_element_type=jnp.float32).astype(
        jnp.bfloat16
    )


def body(
    prompt_pages,
    send_page,
    page_table,
    context_len,
    new_latent,
    queries,
    moe_rows,
    routing,
    gate_weights,
    expert_gate,
    expert_up,
    expert_down,
):
    peers = lax.axis_size("dev")
    pages = prompt_pages[0]
    outgoing_slots = send_page[0]
    page_len, width_lat = (pages.shape[1], pages.shape[2])
    capp = outgoing_slots.shape[0] // peers
    picked_pages = pages[jnp.maximum(outgoing_slots, 0)]
    arrived = lax.all_to_all(
        picked_pages.reshape(peers, capp, page_len, width_lat),
        "dev",
        split_axis=0,
        concat_axis=0,
        tiled=True,
    )
    arrived = arrived.reshape(peers * capp, page_len, width_lat)

    owned = expert_gate.shape[0]
    experts = peers * owned
    rows = routing.shape[1]
    width = moe_rows.shape[2]
    named = routing[0][:, :, None] == jnp.arange(experts)[None, None, :]
    dense = jnp.sum(jnp.where(named, gate_weights[0][:, :, None], 0.0), axis=1)
    high = dense.astype(jnp.bfloat16)
    low = (dense - high.astype(jnp.float32)).astype(jnp.bfloat16)
    extra = jnp.concatenate([high, low], axis=1)
    pad = -extra.shape[1] % 128
    packed = jnp.concatenate([moe_rows[0], jnp.pad(extra, ((0, 0), (0, pad)))], axis=1)
    pooled = lax.all_gather(packed, RANK, axis=0, tiled=True)
    every = pooled[:, :width]
    first = lax.axis_index("dev") * owned
    total = None
    for own in range(owned):
        column = width + first + own
        weight = lax.dynamic_slice_in_dim(pooled, column, 1, 1).astype(jnp.float32) + lax.dynamic_slice_in_dim(
            pooled, column + experts, 1, 1
        ).astype(jnp.float32)
        gate = jnp.dot(every, expert_gate[own], preferred_element_type=jnp.float32)
        up = jnp.dot(every, expert_up[own], preferred_element_type=jnp.float32)
        hidden = (jax.nn.silu(gate) * up).astype(jnp.bfloat16)
        term = jnp.dot(hidden, expert_down[own], preferred_element_type=jnp.float32) * weight
        total = term if total is None else total + term
    mixed = lax.psum_scatter(total.astype(jnp.bfloat16), RANK, scatter_dimension=0, tiled=True)

    table = page_table[0]
    requests, most_pages = table.shape
    cache = arrived[jnp.maximum(table, 0)].reshape(requests, most_pages * page_len, width_lat)
    attended = attend(queries[0], new_latent[0], cache, context_len[0])
    return (attended[None], mixed[None])


def solution(mesh):
    rank = ("grp",) + RANK
    return jax.shard_map(
        body,
        mesh=mesh,
        in_specs=(
            P(rank, None, None, None),
            P(rank, None),
            P(rank, None, None),
            P(rank, None),
            P(rank, None, None, None),
            P(rank, None, None, None, None),
            P(rank, None, None),
            P(rank, None, None),
            P(rank, None, None),
            P("dev", None, ("section", "tp")),
            P("dev", None, ("section", "tp")),
            P("dev", ("section", "tp"), None),
        ),
        out_specs=(
            P(rank, None, None, None, None),
            P(rank, None, None),
        ),
        check_vma=False,
    )
```

```python
import jax
import jax.numpy as jnp
from jax import lax
from jax.sharding import PartitionSpec as P

VDIM = 512
SCALE = 192.0 ** (-0.5)
RANK = ("dev", "section", "tp")


def gather_stages(peers, blocks):
    low = blocks.bit_length() - 1
    bits = peers.bit_length() - 1
    far = [low + bit for bit in range(2, bits)]
    near = list(range(low)) + [low + bit for bit in range(1, min(bits, 2))]
    last = [low + bit for bit in range(min(bits, 1))]
    stages = []
    for group in (far, near, last):
        stages += [group[at : at + 2] for at in range(0, len(group), 2)]
    return stages


def masks_of(stage):
    masks = [0]
    for bit in stage:
        masks += [mask | (1 << bit) for mask in masks]
    return masks


def exchange(value, mask):
    count = lax.axis_size(RANK)
    return lax.ppermute(value, RANK, [(at, at ^ mask) for at in range(count)])


def attend(queries, new_latent, cache, lengths):
    steps = queries.shape[1]
    ctx = cache.shape[1]
    keys = jnp.concatenate([cache, new_latent], axis=1)
    scores = jnp.einsum("rshl,rkl->rshk", queries, keys, preferred_element_type=jnp.float32) * SCALE
    position = jnp.arange(ctx + steps)
    step_index = jnp.arange(steps)
    in_cache = position[None, :] < lengths[:, None]
    in_new = (position[None, :] >= ctx) & (position[None, :] - ctx <= step_index[:, None])
    allowed = in_cache[:, None, :] | in_new[None, :, :]
    scores = jnp.where(allowed[:, :, None, :], scores, -jnp.inf)
    top = jnp.max(scores, axis=-1, keepdims=True)
    weights = jnp.exp(scores - top)
    weights = (weights / jnp.sum(weights, axis=-1, keepdims=True)).astype(jnp.bfloat16)
    values = keys[:, :, :VDIM]
    return jnp.einsum("rshk,rkv->rshv", weights, values, preferred_element_type=jnp.float32).astype(
        jnp.bfloat16
    )


def body(
    prompt_pages,
    send_page,
    page_table,
    context_len,
    new_latent,
    queries,
    moe_rows,
    routing,
    gate_weights,
    expert_gate,
    expert_up,
    expert_down,
):
    peers = lax.axis_size("dev")
    pages = prompt_pages[0]
    outgoing_slots = send_page[0]
    page_len, width_lat = (pages.shape[1], pages.shape[2])
    capp = outgoing_slots.shape[0] // peers
    picked_pages = pages[jnp.maximum(outgoing_slots, 0)]
    arrived = lax.all_to_all(
        picked_pages.reshape(peers, capp, page_len, width_lat),
        "dev",
        split_axis=0,
        concat_axis=0,
        tiled=True,
    )
    arrived = arrived.reshape(peers * capp, page_len, width_lat)

    owned = expert_gate.shape[0]
    experts = peers * owned
    rows = routing.shape[1]
    width = moe_rows.shape[2]
    named = routing[0][:, :, None] == jnp.arange(experts)[None, None, :]
    dense = jnp.sum(jnp.where(named, gate_weights[0][:, :, None], 0.0), axis=1)
    high = dense.astype(jnp.bfloat16)
    low = (dense - high.astype(jnp.float32)).astype(jnp.bfloat16)
    extra = jnp.concatenate([high, low], axis=1)
    pad = -extra.shape[1] % 128
    packed = jnp.concatenate([moe_rows[0], jnp.pad(extra, ((0, 0), (0, pad)))], axis=1)
    stages = gather_stages(peers, lax.axis_size(("section", "tp")))
    pooled = packed
    for stage in stages:
        pooled = jnp.concatenate(
            [pooled] + [exchange(pooled, mask) for mask in masks_of(stage)[1:]], axis=0
        )
    every = pooled[:, :width]
    first = lax.axis_index("dev") * owned
    total = None
    for own in range(owned):
        column = width + first + own
        weight = lax.dynamic_slice_in_dim(pooled, column, 1, 1).astype(jnp.float32) + lax.dynamic_slice_in_dim(
            pooled, column + experts, 1, 1
        ).astype(jnp.float32)
        gate = jnp.dot(every, expert_gate[own], preferred_element_type=jnp.float32)
        up = jnp.dot(every, expert_up[own], preferred_element_type=jnp.float32)
        hidden = (jax.nn.silu(gate) * up).astype(jnp.bfloat16)
        term = jnp.dot(hidden, expert_down[own], preferred_element_type=jnp.float32) * weight
        total = term if total is None else total + term
    mixed = total.astype(jnp.bfloat16)
    for stage in stages[::-1]:
        masks = masks_of(stage)
        count = mixed.shape[0] // len(masks)
        kept = mixed[:count].astype(jnp.float32)
        for turn in range(1, len(masks)):
            sent = mixed[turn * count : (turn + 1) * count]
            kept = kept + exchange(sent, masks[turn]).astype(jnp.float32)
        mixed = kept.astype(jnp.bfloat16)

    table = page_table[0]
    requests, most_pages = table.shape
    cache = arrived[jnp.maximum(table, 0)].reshape(requests, most_pages * page_len, width_lat)
    attended = attend(queries[0], new_latent[0], cache, context_len[0])
    return (attended[None], mixed[None])


def solution(mesh):
    rank = ("grp",) + RANK
    return jax.shard_map(
        body,
        mesh=mesh,
        in_specs=(
            P(rank, None, None, None),
            P(rank, None),
            P(rank, None, None),
            P(rank, None),
            P(rank, None, None, None),
            P(rank, None, None, None, None),
            P(rank, None, None),
            P(rank, None, None),
            P(rank, None, None),
            P("dev", None, ("section", "tp")),
            P("dev", None, ("section", "tp")),
            P("dev", ("section", "tp"), None),
        ),
        out_specs=(
            P(rank, None, None, None, None),
            P(rank, None, None),
        ),
        check_vma=False,
    )
```

```python
import jax
import jax.numpy as jnp
from jax import lax
from jax.sharding import PartitionSpec as P

VDIM = 512
SCALE = 192.0 ** (-0.5)
RANK = ("dev", "section", "tp")


def steps_of(peers, blocks):
    low = blocks.bit_length() - 1
    bits = peers.bit_length() - 1
    far = [low + bit for bit in range(2, bits)]
    near = list(range(low)) + [low + bit for bit in range(1, min(bits, 2))]
    last = [low + bit for bit in range(min(bits, 1))]
    return far, near, last


def exchange(value, bit):
    count = lax.axis_size(RANK)
    return lax.ppermute(value, RANK, [(at, at ^ (1 << bit)) for at in range(count)])


def spread(value, bit):
    return lax.optimization_barrier(jnp.concatenate([value, exchange(value, bit)], axis=0))


def collect(value, bit):
    half = value.shape[0] // 2
    kept = value[:half].astype(jnp.float32) + exchange(value[half:], bit).astype(jnp.float32)
    return kept.astype(jnp.bfloat16)


def attend(queries, new_latent, cache, lengths):
    steps = queries.shape[1]
    ctx = cache.shape[1]
    keys = jnp.concatenate([cache, new_latent], axis=1)
    scores = jnp.einsum("rshl,rkl->rshk", queries, keys, preferred_element_type=jnp.float32) * SCALE
    position = jnp.arange(ctx + steps)
    step_index = jnp.arange(steps)
    in_cache = position[None, :] < lengths[:, None]
    in_new = (position[None, :] >= ctx) & (position[None, :] - ctx <= step_index[:, None])
    allowed = in_cache[:, None, :] | in_new[None, :, :]
    scores = jnp.where(allowed[:, :, None, :], scores, -jnp.inf)
    top = jnp.max(scores, axis=-1, keepdims=True)
    weights = jnp.exp(scores - top)
    weights = (weights / jnp.sum(weights, axis=-1, keepdims=True)).astype(jnp.bfloat16)
    values = keys[:, :, :VDIM]
    return jnp.einsum("rshk,rkv->rshv", weights, values, preferred_element_type=jnp.float32).astype(
        jnp.bfloat16
    )


def body(
    prompt_pages,
    send_page,
    page_table,
    context_len,
    new_latent,
    queries,
    moe_rows,
    routing,
    gate_weights,
    expert_gate,
    expert_up,
    expert_down,
):
    peers = lax.axis_size("dev")
    pages = prompt_pages[0]
    outgoing_slots = send_page[0]
    page_len, width_lat = (pages.shape[1], pages.shape[2])
    capp = outgoing_slots.shape[0] // peers
    picked_pages = pages[jnp.maximum(outgoing_slots, 0)]
    owned = expert_gate.shape[0]
    experts = peers * owned
    rows = routing.shape[1]
    width = moe_rows.shape[2]
    named = routing[0][:, :, None] == jnp.arange(experts)[None, None, :]
    dense = jnp.sum(jnp.where(named, gate_weights[0][:, :, None], 0.0), axis=1)
    high = dense.astype(jnp.bfloat16)
    low = (dense - high.astype(jnp.float32)).astype(jnp.bfloat16)
    extra = jnp.concatenate([high, low], axis=1)
    pad = -extra.shape[1] % 128
    packed = jnp.concatenate([moe_rows[0], jnp.pad(extra, ((0, 0), (0, pad)))], axis=1)
    far, near, last = steps_of(peers, lax.axis_size(("section", "tp")))
    pooled = packed[None]
    for bit in far:
        pooled = spread(pooled, bit)
    half = pooled.shape[0] // 2
    one, two = pooled[:half], pooled[half:]
    for turn, (bit, other) in enumerate(zip(near, near[::-1])):
        if turn == len(near) - 1:
            one, two, picked_pages = lax.optimization_barrier((one, two, picked_pages))
        one, two = spread(one, bit), spread(two, other)
    arrived = lax.all_to_all(
        picked_pages.reshape(peers, capp, page_len, width_lat),
        "dev",
        split_axis=0,
        concat_axis=0,
        tiled=True,
    )
    arrived = arrived.reshape(peers * capp, page_len, width_lat)
    pooled = jnp.concatenate([one, two], axis=0)
    for bit in last:
        pooled = spread(pooled, bit)
    pooled = pooled.reshape(-1, pooled.shape[-1])
    every = pooled[:, :width]
    first = lax.axis_index("dev") * owned
    total = None
    for own in range(owned):
        column = width + first + own
        weight = lax.dynamic_slice_in_dim(pooled, column, 1, 1).astype(jnp.float32) + lax.dynamic_slice_in_dim(
            pooled, column + experts, 1, 1
        ).astype(jnp.float32)
        gate = jnp.dot(every, expert_gate[own], preferred_element_type=jnp.float32)
        up = jnp.dot(every, expert_up[own], preferred_element_type=jnp.float32)
        hidden = (jax.nn.silu(gate) * up).astype(jnp.bfloat16)
        term = jnp.dot(hidden, expert_down[own], preferred_element_type=jnp.float32) * weight
        total = term if total is None else total + term
    mixed = total.astype(jnp.bfloat16).reshape(-1, rows, width)
    for bit in last[::-1]:
        mixed = collect(mixed, bit)
    half = mixed.shape[0] // 2
    one, two = mixed[:half], mixed[half:]
    for bit, other in zip(near[::-1], near):
        one, two = collect(one, bit), collect(two, other)
    mixed = jnp.concatenate([one, two], axis=0)
    for bit in far[::-1]:
        mixed = collect(mixed, bit)
    mixed = mixed[0]

    table = page_table[0]
    requests, most_pages = table.shape
    cache = arrived[jnp.maximum(table, 0)].reshape(requests, most_pages * page_len, width_lat)
    attended = attend(queries[0], new_latent[0], cache, context_len[0])
    return (attended[None], mixed[None])


def solution(mesh):
    rank = ("grp",) + RANK
    return jax.shard_map(
        body,
        mesh=mesh,
        in_specs=(
            P(rank, None, None, None),
            P(rank, None),
            P(rank, None, None),
            P(rank, None),
            P(rank, None, None, None),
            P(rank, None, None, None, None),
            P(rank, None, None),
            P(rank, None, None),
            P(rank, None, None),
            P("dev", None, ("section", "tp")),
            P("dev", None, ("section", "tp")),
            P("dev", ("section", "tp"), None),
        ),
        out_specs=(
            P(rank, None, None, None, None),
            P(rank, None, None),
        ),
        check_vma=False,
    )
```

```python
import jax
import jax.numpy as jnp
from jax import lax
from jax.experimental import pallas as pl
from jax.experimental.pallas import tpu as pltpu
from jax.sharding import PartitionSpec as P

VDIM = 512
SCALE = 192.0 ** (-0.5)
RANK = ("dev", "section", "tp")
VMEM_LIMIT = 48 * 1024 * 1024


def levels_of(peers, blocks):
    low = blocks.bit_length() - 1
    bits = peers.bit_length() - 1
    far = [low + bit for bit in range(2, bits)]
    near = list(range(low)) + [low + bit for bit in range(1, min(bits, 2))]
    last = [low + bit for bit in range(min(bits, 1))]
    return far, near, last


def masks_of(bits):
    masks = [0]
    for bit in bits:
        masks += [mask | (1 << bit) for mask in masks]
    return masks


def exchange(value, mask):
    count = lax.axis_size(RANK)
    return lax.ppermute(value, RANK, [(at, at ^ mask) for at in range(count)])


def swap(value, bits):
    masks = masks_of(bits)
    count = lax.axis_size(RANK)
    groups = [[at | mask for mask in masks] for at in range(count) if not at & masks[-1]]
    return lax.all_to_all(value, RANK, split_axis=0, concat_axis=0, axis_index_groups=groups, tiled=True)


def experts_kernel(
    first_ref, own_ref, got_ref, gate_hbm, up_hbm, down_hbm, kept_ref, sent_ref,
    rows_ref, hidden_ref, gate_ref, up_ref, down_ref, in_sem, down_sem,
):
    count = own_ref.shape[0]
    owned, width, units = gate_hbm.shape
    experts = first_ref[1]
    step = min(units, 256)
    wide = 512 if width % 512 == 0 else 128
    turns, ends = units // step, width // wide

    def load_in(which, own, turn):
        source, target = ((gate_hbm, gate_ref), (up_hbm, up_ref))[which]
        part = (own, slice(None), pl.ds(turn * step, step))
        return pltpu.make_async_copy(source.at[part], target.at[part], in_sem.at[which, own, turn])

    def load_down(own, turn):
        part = (own, slice(None), pl.ds(turn * wide, wide))
        return pltpu.make_async_copy(down_hbm.at[part], down_ref.at[part], down_sem.at[own, turn])

    for own in range(owned):
        for turn in range(turns):
            load_in(0, own, turn).start()
            load_in(1, own, turn).start()
    for turn in range(ends):
        for own in range(owned):
            load_down(own, turn).start()
    rows_ref[:count] = own_ref[...]
    rows_ref[count:] = got_ref[...]
    extra = rows_ref[:, width:].astype(jnp.float32)
    lane = lax.broadcasted_iota(jnp.int32, extra.shape, 1)
    weights = []
    for own in range(owned):
        expert = first_ref[0] + own
        named = (lane == expert) | (lane == expert + experts)
        weights.append(jnp.sum(jnp.where(named, extra, 0.0), axis=1, keepdims=True))
        for turn in range(turns):
            part = pl.ds(turn * step, step)
            x = rows_ref[:, :width]
            load_in(0, own, turn).wait()
            gate = jnp.dot(x, gate_ref[own, :, part], preferred_element_type=jnp.float32)
            load_in(1, own, turn).wait()
            up = jnp.dot(x, up_ref[own, :, part], preferred_element_type=jnp.float32)
            hidden = gate / (1.0 + jnp.exp(-gate)) * up
            hidden_ref[own, :, part] = hidden.astype(jnp.bfloat16)
    for turn in range(ends):
        part = pl.ds(turn * wide, wide)
        total = None
        for own in range(owned):
            load_down(own, turn).wait()
            term = jnp.dot(
                hidden_ref[own], down_ref[own, :, part], preferred_element_type=jnp.float32
            ) * weights[own]
            total = term if total is None else total + term
        total = total.astype(jnp.bfloat16)
        kept_ref[:, part] = total[:count]
        sent_ref[:, part] = total[count:]


def experts_of(own, got, first, experts, expert_gate, expert_up, expert_down):
    count, packed = own.shape
    owned, width, units = expert_gate.shape
    scalars = jnp.stack([first, jnp.int32(experts)])
    vmem = pl.BlockSpec(memory_space=pltpu.VMEM)
    hbm = pl.BlockSpec(memory_space=pltpu.HBM)
    half = jax.ShapeDtypeStruct((count, width), jnp.bfloat16)
    step = min(units, 256)
    wide = 512 if width % 512 == 0 else 128
    return pl.pallas_call(
        experts_kernel,
        out_shape=(half, half),
        in_specs=[pl.BlockSpec(memory_space=pltpu.SMEM), vmem, vmem, hbm, hbm, hbm],
        out_specs=(vmem, vmem),
        scratch_shapes=[
            pltpu.VMEM((2 * count, packed), jnp.bfloat16),
            pltpu.VMEM((owned, 2 * count, units), jnp.bfloat16),
            pltpu.VMEM(expert_gate.shape, jnp.bfloat16),
            pltpu.VMEM(expert_up.shape, jnp.bfloat16),
            pltpu.VMEM(expert_down.shape, jnp.bfloat16),
            pltpu.SemaphoreType.DMA((2, owned, units // step)),
            pltpu.SemaphoreType.DMA((owned, width // wide)),
        ],
        compiler_params=pltpu.CompilerParams(vmem_limit_bytes=VMEM_LIMIT),
        cost_estimate=pl.CostEstimate(
            flops=12 * count * owned * width * units,
            bytes_accessed=6 * owned * width * units,
            transcendentals=2 * count * owned * units,
        ),
        name="experts",
    )(scalars, own, got, expert_gate, expert_up, expert_down)


def attend(queries, new_latent, cache, lengths):
    steps = queries.shape[1]
    ctx = cache.shape[1]
    keys = jnp.concatenate([cache, new_latent], axis=1)
    scores = jnp.einsum("rshl,rkl->rshk", queries, keys, preferred_element_type=jnp.float32) * SCALE
    position = jnp.arange(ctx + steps)
    step_index = jnp.arange(steps)
    in_cache = position[None, :] < lengths[:, None]
    in_new = (position[None, :] >= ctx) & (position[None, :] - ctx <= step_index[:, None])
    allowed = in_cache[:, None, :] | in_new[None, :, :]
    scores = jnp.where(allowed[:, :, None, :], scores, -jnp.inf)
    top = jnp.max(scores, axis=-1, keepdims=True)
    weights = jnp.exp(scores - top)
    weights = (weights / jnp.sum(weights, axis=-1, keepdims=True)).astype(jnp.bfloat16)
    values = keys[:, :, :VDIM]
    return jnp.einsum("rshk,rkv->rshv", weights, values, preferred_element_type=jnp.float32).astype(
        jnp.bfloat16
    )


def body(
    prompt_pages,
    send_page,
    page_table,
    context_len,
    new_latent,
    queries,
    moe_rows,
    routing,
    gate_weights,
    expert_gate,
    expert_up,
    expert_down,
):
    peers = lax.axis_size("dev")
    pages = prompt_pages[0]
    outgoing_slots = send_page[0]
    page_len, width_lat = (pages.shape[1], pages.shape[2])
    capp = outgoing_slots.shape[0] // peers
    picked_pages = pages[jnp.maximum(outgoing_slots, 0)]
    owned = expert_gate.shape[0]
    experts = peers * owned
    rows = routing.shape[1]
    width = moe_rows.shape[2]
    named = routing[0][:, :, None] == jnp.arange(experts)[None, None, :]
    dense = jnp.sum(jnp.where(named, gate_weights[0][:, :, None], 0.0), axis=1)
    high = dense.astype(jnp.bfloat16)
    low = (dense - high.astype(jnp.float32)).astype(jnp.bfloat16)
    extra = jnp.concatenate([high, low], axis=1)
    pad = -extra.shape[1] % 128
    packed = jnp.concatenate([moe_rows[0], jnp.pad(extra, ((0, 0), (0, pad)))], axis=1)
    far, near, last = levels_of(peers, lax.axis_size(("section", "tp")))
    blocks = len(masks_of(far))
    pooled = swap(jnp.broadcast_to(packed, (blocks,) + packed.shape), far)
    pooled = pooled.reshape(blocks * rows, packed.shape[1])
    pooled, picked_pages = lax.optimization_barrier((pooled, picked_pages))
    pooled = jnp.concatenate([pooled] + [exchange(pooled, mask) for mask in masks_of(near)[1:]], axis=0)
    arrived = lax.all_to_all(
        picked_pages.reshape(peers, capp, page_len, width_lat),
        "dev",
        split_axis=0,
        concat_axis=0,
        tiled=True,
    )
    arrived = arrived.reshape(peers * capp, page_len, width_lat)
    pooled = lax.optimization_barrier(pooled)
    other = masks_of(last)[-1]
    first = lax.axis_index("dev") * owned
    kept, sent = experts_of(
        pooled, exchange(pooled, other), first, experts, expert_gate, expert_up, expert_down
    )
    mixed = kept.astype(jnp.float32) + exchange(sent, other).astype(jnp.float32)
    masks = masks_of(near)
    mixed = mixed.astype(jnp.bfloat16).reshape(len(masks), -1, width)
    total = mixed[0].astype(jnp.float32)
    for turn in range(1, len(masks)):
        total = total + exchange(mixed[turn], masks[turn]).astype(jnp.float32)
    mixed = total.astype(jnp.bfloat16).reshape(blocks, rows, width)
    mixed = jnp.sum(swap(mixed, far).astype(jnp.float32), axis=0).astype(jnp.bfloat16)

    table = page_table[0]
    requests, most_pages = table.shape
    cache = arrived[jnp.maximum(table, 0)].reshape(requests, most_pages * page_len, width_lat)
    attended = attend(queries[0], new_latent[0], cache, context_len[0])
    return (attended[None], mixed[None])


def solution(mesh):
    rank = ("grp",) + RANK
    return jax.shard_map(
        body,
        mesh=mesh,
        in_specs=(
            P(rank, None, None, None),
            P(rank, None),
            P(rank, None, None),
            P(rank, None),
            P(rank, None, None, None),
            P(rank, None, None, None, None),
            P(rank, None, None),
            P(rank, None, None),
            P(rank, None, None),
            P("dev", None, ("section", "tp")),
            P("dev", None, ("section", "tp")),
            P("dev", ("section", "tp"), None),
        ),
        out_specs=(
            P(rank, None, None, None, None),
            P(rank, None, None),
        ),
        check_vma=False,
    )
```

```python
import jax
import jax.numpy as jnp
from jax import lax
from jax.experimental import pallas as pl
from jax.experimental.pallas import tpu as pltpu
from jax.sharding import PartitionSpec as P

VDIM = 512
SCALE = 192.0 ** (-0.5)
RANK = ("dev", "section", "tp")
VMEM_LIMIT = 50 * 1024 * 1024


def levels_of(peers, blocks):
    low = blocks.bit_length() - 1
    bits = peers.bit_length() - 1
    far = [low + bit for bit in range(2, bits)]
    near = list(range(low)) + [low + bit for bit in range(1, min(bits, 2))]
    last = [low + bit for bit in range(min(bits, 1))]
    return far, near, last


def masks_of(bits):
    masks = [0]
    for bit in bits:
        masks += [mask | (1 << bit) for mask in masks]
    return masks


def exchange(value, mask):
    count = lax.axis_size(RANK)
    return lax.ppermute(value, RANK, [(at, at ^ mask) for at in range(count)])


def pairs_of(bits):
    return [bits[at : at + 2] for at in range(0, len(bits), 2)]


def collect(value, bits):
    masks = masks_of(bits)
    count = value.shape[0] // len(masks)
    total = value[:count].astype(jnp.float32)
    for turn in range(1, len(masks)):
        sent = value[turn * count : (turn + 1) * count]
        total = total + exchange(sent, masks[turn]).astype(jnp.float32)
    return total.astype(jnp.bfloat16)


def experts_kernel(
    first_ref, own_ref, got_ref, gate_hbm, up_hbm, down_hbm, kept_ref, sent_ref,
    rows_ref, hidden_ref, gate_ref, up_ref, down_ref, in_sem, down_sem,
):
    count = own_ref.shape[0]
    owned, width, units = gate_hbm.shape
    experts = first_ref[1]
    step = min(units, 256)
    wide = 512 if width % 512 == 0 else 128
    turns, ends = units // step, width // wide

    def load_in(which, own, turn):
        source, target = ((gate_hbm, gate_ref), (up_hbm, up_ref))[which]
        part = (own, slice(None), pl.ds(turn * step, step))
        return pltpu.make_async_copy(source.at[part], target.at[part], in_sem.at[which, own, turn])

    def load_down(own, turn):
        part = (own, slice(None), pl.ds(turn * wide, wide))
        return pltpu.make_async_copy(down_hbm.at[part], down_ref.at[part], down_sem.at[own, turn])

    for own in range(owned):
        for turn in range(turns):
            load_in(0, own, turn).start()
            load_in(1, own, turn).start()
    for turn in range(ends):
        for own in range(owned):
            load_down(own, turn).start()
    rows_ref[:count] = own_ref[...]
    rows_ref[count:] = got_ref[...]
    extra = rows_ref[:, width:].astype(jnp.float32)
    lane = lax.broadcasted_iota(jnp.int32, extra.shape, 1)
    weights = []
    for own in range(owned):
        expert = first_ref[0] + own
        named = (lane == expert) | (lane == expert + experts)
        weights.append(jnp.sum(jnp.where(named, extra, 0.0), axis=1, keepdims=True))
        for turn in range(turns):
            part = pl.ds(turn * step, step)
            x = rows_ref[:, :width]
            load_in(0, own, turn).wait()
            gate = jnp.dot(x, gate_ref[own, :, part], preferred_element_type=jnp.float32)
            load_in(1, own, turn).wait()
            up = jnp.dot(x, up_ref[own, :, part], preferred_element_type=jnp.float32)
            hidden = gate / (1.0 + jnp.exp(-gate)) * up
            hidden_ref[own, :, part] = hidden.astype(jnp.bfloat16)
    for turn in range(ends):
        part = pl.ds(turn * wide, wide)
        total = None
        for own in range(owned):
            load_down(own, turn).wait()
            term = jnp.dot(
                hidden_ref[own], down_ref[own, :, part], preferred_element_type=jnp.float32
            ) * weights[own]
            total = term if total is None else total + term
        total = total.astype(jnp.bfloat16)
        kept_ref[:, part] = total[:count]
        sent_ref[:, part] = total[count:]


def experts_of(own, got, first, experts, expert_gate, expert_up, expert_down):
    count, packed = own.shape
    owned, width, units = expert_gate.shape
    scalars = jnp.stack([first, jnp.int32(experts)])
    vmem = pl.BlockSpec(memory_space=pltpu.VMEM)
    hbm = pl.BlockSpec(memory_space=pltpu.HBM)
    half = jax.ShapeDtypeStruct((count, width), jnp.bfloat16)
    step = min(units, 256)
    wide = 512 if width % 512 == 0 else 128
    return pl.pallas_call(
        experts_kernel,
        out_shape=(half, half),
        in_specs=[pl.BlockSpec(memory_space=pltpu.SMEM), vmem, vmem, hbm, hbm, hbm],
        out_specs=(vmem, vmem),
        scratch_shapes=[
            pltpu.VMEM((2 * count, packed), jnp.bfloat16),
            pltpu.VMEM((owned, 2 * count, units), jnp.bfloat16),
            pltpu.VMEM(expert_gate.shape, jnp.bfloat16),
            pltpu.VMEM(expert_up.shape, jnp.bfloat16),
            pltpu.VMEM(expert_down.shape, jnp.bfloat16),
            pltpu.SemaphoreType.DMA((2, owned, units // step)),
            pltpu.SemaphoreType.DMA((owned, width // wide)),
        ],
        compiler_params=pltpu.CompilerParams(vmem_limit_bytes=VMEM_LIMIT),
        cost_estimate=pl.CostEstimate(
            flops=48 * count * owned * width * units,
            bytes_accessed=6 * owned * width * units,
            transcendentals=2 * count * owned * units,
        ),
        name="experts",
    )(scalars, own, got, expert_gate, expert_up, expert_down)


def attend(queries, new_latent, cache, lengths):
    steps = queries.shape[1]
    ctx = cache.shape[1]
    keys = jnp.concatenate([cache, new_latent], axis=1)
    scores = jnp.einsum("rshl,rkl->rshk", queries, keys, preferred_element_type=jnp.float32) * SCALE
    position = jnp.arange(ctx + steps)
    step_index = jnp.arange(steps)
    in_cache = position[None, :] < lengths[:, None]
    in_new = (position[None, :] >= ctx) & (position[None, :] - ctx <= step_index[:, None])
    allowed = in_cache[:, None, :] | in_new[None, :, :]
    scores = jnp.where(allowed[:, :, None, :], scores, -jnp.inf)
    top = jnp.max(scores, axis=-1, keepdims=True)
    weights = jnp.exp(scores - top)
    weights = (weights / jnp.sum(weights, axis=-1, keepdims=True)).astype(jnp.bfloat16)
    values = keys[:, :, :VDIM]
    return jnp.einsum("rshk,rkv->rshv", weights, values, preferred_element_type=jnp.float32).astype(
        jnp.bfloat16
    )


def body(
    prompt_pages,
    send_page,
    page_table,
    context_len,
    new_latent,
    queries,
    moe_rows,
    routing,
    gate_weights,
    expert_gate,
    expert_up,
    expert_down,
):
    peers = lax.axis_size("dev")
    pages = prompt_pages[0]
    outgoing_slots = send_page[0]
    page_len, width_lat = (pages.shape[1], pages.shape[2])
    capp = outgoing_slots.shape[0] // peers
    picked_pages = pages[jnp.maximum(outgoing_slots, 0)]
    owned = expert_gate.shape[0]
    experts = peers * owned
    rows = routing.shape[1]
    width = moe_rows.shape[2]
    named = routing[0][:, :, None] == jnp.arange(experts)[None, None, :]
    dense = jnp.sum(jnp.where(named, gate_weights[0][:, :, None], 0.0), axis=1)
    high = dense.astype(jnp.bfloat16)
    low = (dense - high.astype(jnp.float32)).astype(jnp.bfloat16)
    extra = jnp.concatenate([high, low], axis=1)
    pad = -extra.shape[1] % 128
    packed = jnp.concatenate([moe_rows[0], jnp.pad(extra, ((0, 0), (0, pad)))], axis=1)
    far, near, last = levels_of(peers, lax.axis_size(("section", "tp")))
    pooled = packed[None]
    for bits in pairs_of(far):
        pooled = jnp.concatenate([pooled] + [exchange(pooled, mask) for mask in masks_of(bits)[1:]], axis=0)
    pooled = lax.optimization_barrier(pooled).reshape(-1, packed.shape[1])
    pooled, picked_pages = lax.optimization_barrier((pooled, picked_pages))
    pooled = jnp.concatenate([pooled] + [exchange(pooled, mask) for mask in masks_of(near)[1:]], axis=0)
    arrived = lax.all_to_all(
        picked_pages.reshape(peers, capp, page_len, width_lat),
        "dev",
        split_axis=0,
        concat_axis=0,
        tiled=True,
    )
    arrived = arrived.reshape(peers * capp, page_len, width_lat)
    pooled = lax.optimization_barrier(pooled)
    other = masks_of(last)[-1]
    first = lax.axis_index("dev") * owned
    kept, sent = experts_of(
        pooled, exchange(pooled, other), first, experts, expert_gate, expert_up, expert_down
    )
    mixed = kept.astype(jnp.float32) + exchange(sent, other).astype(jnp.float32)
    mixed, arrived = lax.optimization_barrier((mixed.astype(jnp.bfloat16), arrived))
    for bits in [near] + pairs_of(far)[::-1]:
        mixed = collect(mixed, bits)

    table = page_table[0]
    requests, most_pages = table.shape
    cache = arrived[jnp.maximum(table, 0)].reshape(requests, most_pages * page_len, width_lat)
    attended = attend(queries[0], new_latent[0], cache, context_len[0])
    return (attended[None], mixed[None])


def solution(mesh):
    rank = ("grp",) + RANK
    return jax.shard_map(
        body,
        mesh=mesh,
        in_specs=(
            P(rank, None, None, None),
            P(rank, None),
            P(rank, None, None),
            P(rank, None),
            P(rank, None, None, None),
            P(rank, None, None, None, None),
            P(rank, None, None),
            P(rank, None, None),
            P(rank, None, None),
            P("dev", None, ("section", "tp")),
            P("dev", None, ("section", "tp")),
            P("dev", ("section", "tp"), None),
        ),
        out_specs=(
            P(rank, None, None, None, None),
            P(rank, None, None),
        ),
        check_vma=False,
    )
```

```python
import functools
import jax
import jax.numpy as jnp
from jax import lax
from jax.experimental import pallas as pl
from jax.experimental.pallas import tpu as pltpu
from jax.sharding import PartitionSpec as P

VDIM = 512
SCALE = 192.0 ** (-0.5)
RANK = ("dev", "section", "tp")
VMEM_LIMIT = 50 * 1024 * 1024


def levels_of(peers, blocks):
    low = blocks.bit_length() - 1
    bits = peers.bit_length() - 1
    far = [low + bit for bit in range(2, bits)]
    near = list(range(low)) + [low + bit for bit in range(1, min(bits, 2))]
    last = [low + bit for bit in range(min(bits, 1))]
    return far, near, last


def masks_of(bits):
    masks = [0]
    for bit in bits:
        masks += [mask | (1 << bit) for mask in masks]
    return masks


def exchange(value, mask):
    count = lax.axis_size(RANK)
    return lax.ppermute(value, RANK, [(at, at ^ mask) for at in range(count)])


def pairs_of(bits):
    return [bits[at : at + 2] for at in range(0, len(bits), 2)]


def collect(value, bits):
    masks = masks_of(bits)
    count = value.shape[0] // len(masks)
    total = value[:count].astype(jnp.float32)
    for turn in range(1, len(masks)):
        sent = value[turn * count : (turn + 1) * count]
        total = total + exchange(sent, masks[turn]).astype(jnp.float32)
    return total.astype(jnp.bfloat16)


def experts_kernel(
    first_ref, own_ref, got_ref, gate_hbm, up_hbm, down_hbm, kept_ref, sent_ref,
    rows_ref, hidden_ref, gate_ref, up_ref, down_ref, in_sem, down_sem,
):
    count = own_ref.shape[0]
    owned, width, units = gate_hbm.shape
    experts = first_ref[1]
    step = min(units, 256)
    wide = 512 if width % 512 == 0 else 128
    turns, ends = units // step, width // wide

    def load_in(which, own, turn):
        source, target = ((gate_hbm, gate_ref), (up_hbm, up_ref))[which]
        part = (own, slice(None), pl.ds(turn * step, step))
        return pltpu.make_async_copy(source.at[part], target.at[part], in_sem.at[which, own, turn])

    def load_down(own, turn):
        part = (own, slice(None), pl.ds(turn * wide, wide))
        return pltpu.make_async_copy(down_hbm.at[part], down_ref.at[part], down_sem.at[own, turn])

    for own in range(owned):
        for turn in range(turns):
            load_in(0, own, turn).start()
            load_in(1, own, turn).start()
    for turn in range(ends):
        for own in range(owned):
            load_down(own, turn).start()
    rows_ref[:count] = own_ref[...]
    rows_ref[count:] = got_ref[...]
    extra = rows_ref[:, width:].astype(jnp.float32)
    lane = lax.broadcasted_iota(jnp.int32, extra.shape, 1)
    weights = []
    for own in range(owned):
        expert = first_ref[0] + own
        named = (lane == expert) | (lane == expert + experts)
        weights.append(jnp.sum(jnp.where(named, extra, 0.0), axis=1, keepdims=True))
        for turn in range(turns):
            part = pl.ds(turn * step, step)
            x = rows_ref[:, :width]
            load_in(0, own, turn).wait()
            gate = jnp.dot(x, gate_ref[own, :, part], preferred_element_type=jnp.float32)
            load_in(1, own, turn).wait()
            up = jnp.dot(x, up_ref[own, :, part], preferred_element_type=jnp.float32)
            hidden = gate / (1.0 + jnp.exp(-gate)) * up
            hidden_ref[own, :, part] = hidden.astype(jnp.bfloat16)
    for turn in range(ends):
        part = pl.ds(turn * wide, wide)
        total = None
        for own in range(owned):
            load_down(own, turn).wait()
            term = jnp.dot(
                hidden_ref[own], down_ref[own, :, part], preferred_element_type=jnp.float32
            ) * weights[own]
            total = term if total is None else total + term
        total = total.astype(jnp.bfloat16)
        kept_ref[:, part] = total[:count]
        sent_ref[:, part] = total[count:]


def experts_of(own, got, first, experts, expert_gate, expert_up, expert_down):
    count, packed = own.shape
    owned, width, units = expert_gate.shape
    scalars = jnp.stack([first, jnp.int32(experts)])
    vmem = pl.BlockSpec(memory_space=pltpu.VMEM)
    hbm = pl.BlockSpec(memory_space=pltpu.HBM)
    half = jax.ShapeDtypeStruct((count, width), jnp.bfloat16)
    step = min(units, 256)
    wide = 512 if width % 512 == 0 else 128
    return pl.pallas_call(
        experts_kernel,
        out_shape=(half, half),
        in_specs=[pl.BlockSpec(memory_space=pltpu.SMEM), vmem, vmem, hbm, hbm, hbm],
        out_specs=(vmem, vmem),
        scratch_shapes=[
            pltpu.VMEM((2 * count, packed), jnp.bfloat16),
            pltpu.VMEM((owned, 2 * count, units), jnp.bfloat16),
            pltpu.VMEM(expert_gate.shape, jnp.bfloat16),
            pltpu.VMEM(expert_up.shape, jnp.bfloat16),
            pltpu.VMEM(expert_down.shape, jnp.bfloat16),
            pltpu.SemaphoreType.DMA((2, owned, units // step)),
            pltpu.SemaphoreType.DMA((owned, width // wide)),
        ],
        compiler_params=pltpu.CompilerParams(vmem_limit_bytes=VMEM_LIMIT),
        cost_estimate=pl.CostEstimate(
            flops=48 * count * owned * width * units,
            bytes_accessed=6 * owned * width * units,
            transcendentals=2 * count * owned * units,
        ),
        name="experts",
    )(scalars, own, got, expert_gate, expert_up, expert_down)


def pick_kernel(capp, me_ref, send_ref, pages_ref, out_ref, sems):
    copies = []
    for at in range(out_ref.shape[0]):
        slot = ((at // capp) ^ me_ref[0]) * capp + at % capp
        page = jnp.maximum(send_ref[slot], 0)
        copies.append(pltpu.make_async_copy(pages_ref.at[page], out_ref.at[at], sems.at[at]))
        copies[-1].start()
    for copy in copies:
        copy.wait()


def pick_pages(pages, outgoing_slots, me, capp):
    slots = outgoing_slots.shape[0]
    smem = pl.BlockSpec(memory_space=pltpu.SMEM)
    return pl.pallas_call(
        functools.partial(pick_kernel, capp),
        out_shape=jax.ShapeDtypeStruct((slots,) + pages.shape[1:], pages.dtype),
        in_specs=[smem, smem, pl.BlockSpec(memory_space=pl.ANY)],
        out_specs=pl.BlockSpec(memory_space=pltpu.VMEM),
        scratch_shapes=[pltpu.SemaphoreType.DMA((slots,))],
        cost_estimate=pl.CostEstimate(flops=0, bytes_accessed=4 * pages[0].size * slots, transcendentals=0),
        name="pick",
    )(me.reshape(1), outgoing_slots, pages)


def attend(queries, new_latent, cache, lengths):
    steps = queries.shape[1]
    ctx = cache.shape[1]
    keys = jnp.concatenate([cache, new_latent], axis=1)
    scores = jnp.einsum("rshl,rkl->rshk", queries, keys, preferred_element_type=jnp.float32) * SCALE
    position = jnp.arange(ctx + steps)
    step_index = jnp.arange(steps)
    in_cache = position[None, :] < lengths[:, None]
    in_new = (position[None, :] >= ctx) & (position[None, :] - ctx <= step_index[:, None])
    allowed = in_cache[:, None, :] | in_new[None, :, :]
    scores = jnp.where(allowed[:, :, None, :], scores, -jnp.inf)
    top = jnp.max(scores, axis=-1, keepdims=True)
    weights = jnp.exp(scores - top)
    weights = (weights / jnp.sum(weights, axis=-1, keepdims=True)).astype(jnp.bfloat16)
    values = keys[:, :, :VDIM]
    return jnp.einsum("rshk,rkv->rshv", weights, values, preferred_element_type=jnp.float32).astype(
        jnp.bfloat16
    )


def body(
    prompt_pages,
    send_page,
    page_table,
    context_len,
    new_latent,
    queries,
    moe_rows,
    routing,
    gate_weights,
    expert_gate,
    expert_up,
    expert_down,
):
    peers = lax.axis_size("dev")
    pages = prompt_pages[0]
    outgoing_slots = send_page[0]
    page_len, width_lat = (pages.shape[1], pages.shape[2])
    capp = outgoing_slots.shape[0] // peers
    me = lax.axis_index("dev")
    sent_pages = pick_pages(pages, outgoing_slots, me, capp)
    owned = expert_gate.shape[0]
    experts = peers * owned
    rows = routing.shape[1]
    width = moe_rows.shape[2]
    named = routing[0][:, :, None] == jnp.arange(experts)[None, None, :]
    dense = jnp.sum(jnp.where(named, gate_weights[0][:, :, None], 0.0), axis=1)
    high = dense.astype(jnp.bfloat16)
    low = (dense - high.astype(jnp.float32)).astype(jnp.bfloat16)
    extra = jnp.concatenate([high, low], axis=1)
    pad = -extra.shape[1] % 128
    packed = jnp.concatenate([moe_rows[0], jnp.pad(extra, ((0, 0), (0, pad)))], axis=1)
    blocks = lax.axis_size(("section", "tp"))
    far, near, last = levels_of(peers, blocks)
    low = blocks.bit_length() - 1
    middle = near[low:]
    ends = [1 << len(far), 1 << len(middle), 1 << len(last)]
    moving = sent_pages.reshape(ends + [-1, width_lat])
    for bit in middle:
        moving = jnp.stack([moving[:, 0], exchange(moving[:, 1], 1 << bit)], axis=1)
    pooled = packed[None]
    for bits in pairs_of(far):
        pooled = jnp.concatenate([pooled] + [exchange(pooled, mask) for mask in masks_of(bits)[1:]], axis=0)
    pooled, moving = lax.optimization_barrier((pooled, moving))
    pooled = pooled.reshape(-1, packed.shape[1])
    masks = masks_of(far)
    early = [exchange(moving[turn], masks[turn]) for turn in range(1, len(masks) - 1)]
    pooled = jnp.concatenate([pooled] + [exchange(pooled, mask) for mask in masks_of(near)[1:]], axis=0)
    pooled, early, moving = lax.optimization_barrier((pooled, early, moving))
    late = [exchange(moving[turn], masks[turn]) for turn in range(max(1, len(masks) - 1), len(masks))]
    other = masks_of(last)[-1]
    first = me * owned
    kept, sent = experts_of(
        pooled, exchange(pooled, other), first, experts, expert_gate, expert_up, expert_down
    )
    kept, sent, late = lax.optimization_barrier((kept, sent, late))
    mixed = kept.astype(jnp.float32) + exchange(sent, other).astype(jnp.float32)
    mixed, late = lax.optimization_barrier((mixed.astype(jnp.bfloat16), late))
    moving = jnp.stack([moving[0]] + list(early) + list(late), axis=0)
    for bit in last:
        moving = jnp.stack([moving[:, :, 0], exchange(moving[:, :, 1], 1 << bit)], axis=2)
    mixed = collect(mixed, near)
    mixed, moving = lax.optimization_barrier((mixed, moving))
    for bits in pairs_of(far)[::-1]:
        mixed = collect(mixed, bits)
    arrived = moving.reshape(peers * capp, page_len, width_lat)

    table = page_table[0]
    requests, most_pages = table.shape
    slots = jnp.maximum(table, 0)
    slots = ((slots // capp) ^ me) * capp + slots % capp
    cache = arrived[slots].reshape(requests, most_pages * page_len, width_lat)
    attended = attend(queries[0], new_latent[0], cache, context_len[0])
    return (attended[None], mixed[None])


def solution(mesh):
    rank = ("grp",) + RANK
    return jax.shard_map(
        body,
        mesh=mesh,
        in_specs=(
            P(rank, None, None, None),
            P(rank, None),
            P(rank, None, None),
            P(rank, None),
            P(rank, None, None, None),
            P(rank, None, None, None, None),
            P(rank, None, None),
            P(rank, None, None),
            P(rank, None, None),
            P("dev", None, ("section", "tp")),
            P("dev", None, ("section", "tp")),
            P("dev", ("section", "tp"), None),
        ),
        out_specs=(
            P(rank, None, None, None, None),
            P(rank, None, None),
        ),
        check_vma=False,
    )
```

```python
import jax
import jax.numpy as jnp
from jax import lax
from jax.experimental import pallas as pl
from jax.experimental.pallas import tpu as pltpu
from jax.sharding import PartitionSpec as P

VDIM = 512
SCALE = 192.0 ** (-0.5)
RANK = ("dev", "section", "tp")
VMEM_LIMIT = 50 * 1024 * 1024


def levels_of(peers, blocks):
    low = blocks.bit_length() - 1
    bits = peers.bit_length() - 1
    far = [low + bit for bit in range(2, bits)]
    near = list(range(low)) + [low + bit for bit in range(1, min(bits, 2))]
    last = [low + bit for bit in range(min(bits, 1))]
    return far, near, last


def masks_of(bits):
    masks = [0]
    for bit in bits:
        masks += [mask | (1 << bit) for mask in masks]
    return masks


def exchange(value, mask):
    count = lax.axis_size(RANK)
    return lax.ppermute(value, RANK, [(at, at ^ mask) for at in range(count)])


def pairs_of(bits):
    return [bits[at : at + 2] for at in range(0, len(bits), 2)]


def collect(value, bits):
    masks = masks_of(bits)
    count = value.shape[0] // len(masks)
    total = value[:count].astype(jnp.float32)
    for turn in range(1, len(masks)):
        sent = value[turn * count : (turn + 1) * count]
        total = total + exchange(sent, masks[turn]).astype(jnp.float32)
    return total.astype(jnp.bfloat16)


def experts_kernel(
    first_ref, own_ref, got_ref, gate_hbm, up_hbm, down_hbm, kept_ref, sent_ref,
    rows_ref, hidden_ref, gate_ref, up_ref, down_ref, in_sem, down_sem,
):
    count = own_ref.shape[0]
    owned, width, units = gate_hbm.shape
    experts = first_ref[1]
    step = min(units, 256)
    wide = 512 if width % 512 == 0 else 128
    turns, ends = units // step, width // wide

    def load_in(which, own, turn):
        source, target = ((gate_hbm, gate_ref), (up_hbm, up_ref))[which]
        part = (own, slice(None), pl.ds(turn * step, step))
        return pltpu.make_async_copy(source.at[part], target.at[part], in_sem.at[which, own, turn])

    def load_down(own, turn):
        part = (own, slice(None), pl.ds(turn * wide, wide))
        return pltpu.make_async_copy(down_hbm.at[part], down_ref.at[part], down_sem.at[own, turn])

    for own in range(owned):
        for turn in range(turns):
            load_in(0, own, turn).start()
            load_in(1, own, turn).start()
    for turn in range(ends):
        for own in range(owned):
            load_down(own, turn).start()
    rows_ref[:count] = own_ref[...]
    rows_ref[count:] = got_ref[...]
    extra = rows_ref[:, width:].astype(jnp.float32)
    lane = lax.broadcasted_iota(jnp.int32, extra.shape, 1)
    weights = []
    for own in range(owned):
        expert = first_ref[0] + own
        named = (lane == expert) | (lane == expert + experts)
        weights.append(jnp.sum(jnp.where(named, extra, 0.0), axis=1, keepdims=True))
        for turn in range(turns):
            part = pl.ds(turn * step, step)
            x = rows_ref[:, :width]
            load_in(0, own, turn).wait()
            gate = jnp.dot(x, gate_ref[own, :, part], preferred_element_type=jnp.float32)
            load_in(1, own, turn).wait()
            up = jnp.dot(x, up_ref[own, :, part], preferred_element_type=jnp.float32)
            hidden = gate / (1.0 + jnp.exp(-gate)) * up
            hidden_ref[own, :, part] = hidden.astype(jnp.bfloat16)
    for turn in range(ends):
        part = pl.ds(turn * wide, wide)
        total = None
        for own in range(owned):
            load_down(own, turn).wait()
            term = jnp.dot(
                hidden_ref[own], down_ref[own, :, part], preferred_element_type=jnp.float32
            ) * weights[own]
            total = term if total is None else total + term
        total = total.astype(jnp.bfloat16)
        kept_ref[:, part] = total[:count]
        sent_ref[:, part] = total[count:]


def experts_of(own, got, first, experts, expert_gate, expert_up, expert_down):
    count, packed = own.shape
    owned, width, units = expert_gate.shape
    scalars = jnp.stack([first, jnp.int32(experts)])
    vmem = pl.BlockSpec(memory_space=pltpu.VMEM)
    hbm = pl.BlockSpec(memory_space=pltpu.HBM)
    half = jax.ShapeDtypeStruct((count, width), jnp.bfloat16)
    step = min(units, 256)
    wide = 512 if width % 512 == 0 else 128
    return pl.pallas_call(
        experts_kernel,
        out_shape=(half, half),
        in_specs=[pl.BlockSpec(memory_space=pltpu.SMEM), vmem, vmem, hbm, hbm, hbm],
        out_specs=(vmem, vmem),
        scratch_shapes=[
            pltpu.VMEM((2 * count, packed), jnp.bfloat16),
            pltpu.VMEM((owned, 2 * count, units), jnp.bfloat16),
            pltpu.VMEM(expert_gate.shape, jnp.bfloat16),
            pltpu.VMEM(expert_up.shape, jnp.bfloat16),
            pltpu.VMEM(expert_down.shape, jnp.bfloat16),
            pltpu.SemaphoreType.DMA((2, owned, units // step)),
            pltpu.SemaphoreType.DMA((owned, width // wide)),
        ],
        compiler_params=pltpu.CompilerParams(vmem_limit_bytes=VMEM_LIMIT),
        cost_estimate=pl.CostEstimate(
            flops=48 * count * owned * width * units,
            bytes_accessed=6 * owned * width * units,
            transcendentals=2 * count * owned * units,
        ),
        name="experts",
    )(scalars, own, got, expert_gate, expert_up, expert_down)


def attend(queries, new_latent, cache, lengths):
    steps = queries.shape[1]
    ctx = cache.shape[1]
    keys = jnp.concatenate([cache, new_latent], axis=1)
    scores = jnp.einsum("rshl,rkl->rshk", queries, keys, preferred_element_type=jnp.float32) * SCALE
    position = jnp.arange(ctx + steps)
    step_index = jnp.arange(steps)
    in_cache = position[None, :] < lengths[:, None]
    in_new = (position[None, :] >= ctx) & (position[None, :] - ctx <= step_index[:, None])
    allowed = in_cache[:, None, :] | in_new[None, :, :]
    scores = jnp.where(allowed[:, :, None, :], scores, -jnp.inf)
    top = jnp.max(scores, axis=-1, keepdims=True)
    weights = jnp.exp(scores - top)
    weights = (weights / jnp.sum(weights, axis=-1, keepdims=True)).astype(jnp.bfloat16)
    values = keys[:, :, :VDIM]
    return jnp.einsum("rshk,rkv->rshv", weights, values, preferred_element_type=jnp.float32).astype(
        jnp.bfloat16
    )


def body(
    prompt_pages,
    send_page,
    page_table,
    context_len,
    new_latent,
    queries,
    moe_rows,
    routing,
    gate_weights,
    expert_gate,
    expert_up,
    expert_down,
):
    peers = lax.axis_size("dev")
    pages = prompt_pages[0]
    outgoing_slots = send_page[0]
    page_len, width_lat = (pages.shape[1], pages.shape[2])
    capp = outgoing_slots.shape[0] // peers
    picked_pages = pages[jnp.maximum(outgoing_slots, 0)]
    owned = expert_gate.shape[0]
    experts = peers * owned
    rows = routing.shape[1]
    width = moe_rows.shape[2]
    named = routing[0][:, :, None] == jnp.arange(experts)[None, None, :]
    dense = jnp.sum(jnp.where(named, gate_weights[0][:, :, None], 0.0), axis=1)
    high = dense.astype(jnp.bfloat16)
    low = (dense - high.astype(jnp.float32)).astype(jnp.bfloat16)
    extra = jnp.concatenate([high, low], axis=1)
    pad = -extra.shape[1] % 128
    packed = jnp.concatenate([moe_rows[0], jnp.pad(extra, ((0, 0), (0, pad)))], axis=1)
    far, near, last = levels_of(peers, lax.axis_size(("section", "tp")))
    pooled = packed[None]
    for bits in pairs_of(far):
        pooled = jnp.concatenate([pooled] + [exchange(pooled, mask) for mask in masks_of(bits)[1:]], axis=0)
    pooled = pooled.reshape(-1, packed.shape[1])
    pooled = jnp.concatenate([pooled] + [exchange(pooled, mask) for mask in masks_of(near)[1:]], axis=0)
    arrived = lax.all_to_all(
        picked_pages.reshape(peers, capp, page_len, width_lat),
        "dev",
        split_axis=0,
        concat_axis=0,
        tiled=True,
    )
    arrived = arrived.reshape(peers * capp, page_len, width_lat)
    other = masks_of(last)[-1]
    first = lax.axis_index("dev") * owned
    kept, sent = experts_of(
        pooled, exchange(pooled, other), first, experts, expert_gate, expert_up, expert_down
    )
    mixed = kept.astype(jnp.float32) + exchange(sent, other).astype(jnp.float32)
    mixed = mixed.astype(jnp.bfloat16)
    for bits in [near] + pairs_of(far)[::-1]:
        mixed = collect(mixed, bits)

    table = page_table[0]
    requests, most_pages = table.shape
    cache = arrived[jnp.maximum(table, 0)].reshape(requests, most_pages * page_len, width_lat)
    attended = attend(queries[0], new_latent[0], cache, context_len[0])
    return (attended[None], mixed[None])


def solution(mesh):
    rank = ("grp",) + RANK
    return jax.shard_map(
        body,
        mesh=mesh,
        in_specs=(
            P(rank, None, None, None),
            P(rank, None),
            P(rank, None, None),
            P(rank, None),
            P(rank, None, None, None),
            P(rank, None, None, None, None),
            P(rank, None, None),
            P(rank, None, None),
            P(rank, None, None),
            P("dev", None, ("section", "tp")),
            P("dev", None, ("section", "tp")),
            P("dev", ("section", "tp"), None),
        ),
        out_specs=(
            P(rank, None, None, None, None),
            P(rank, None, None),
        ),
        check_vma=False,
    )
```

```python
import jax
import jax.numpy as jnp
from jax import lax
from jax.experimental import pallas as pl
from jax.experimental.pallas import tpu as pltpu
from jax.sharding import PartitionSpec as P

VDIM = 512
SCALE = 192.0 ** (-0.5)
RANK = ("dev", "section", "tp")
VMEM_LIMIT = 50 * 1024 * 1024


def levels_of(peers, blocks):
    low = blocks.bit_length() - 1
    bits = peers.bit_length() - 1
    far = [low + bit for bit in range(2, bits)]
    near = list(range(low)) + [low + bit for bit in range(1, min(bits, 2))]
    last = [low + bit for bit in range(min(bits, 1))]
    return far, near, last


def masks_of(bits):
    masks = [0]
    for bit in bits:
        masks += [mask | (1 << bit) for mask in masks]
    return masks


def exchange(value, mask):
    count = lax.axis_size(RANK)
    return lax.ppermute(value, RANK, [(at, at ^ mask) for at in range(count)])


def pairs_of(bits):
    return [bits[at : at + 2] for at in range(0, len(bits), 2)]


def collect(value, bits):
    masks = masks_of(bits)
    count = value.shape[0] // len(masks)
    total = value[:count].astype(jnp.float32)
    for turn in range(1, len(masks)):
        sent = value[turn * count : (turn + 1) * count]
        total = total + exchange(sent, masks[turn]).astype(jnp.float32)
    return total.astype(jnp.bfloat16)


def experts_kernel(
    first_ref, own_ref, got_ref, gate_hbm, up_hbm, down_hbm, kept_ref, sent_ref,
    rows_ref, hidden_ref, gate_ref, up_ref, down_ref, in_sem, down_sem,
):
    count = own_ref.shape[0]
    owned, width, units = gate_hbm.shape
    experts = first_ref[1]
    step = min(units, 256)
    wide = 512 if width % 512 == 0 else 128
    turns, ends = units // step, width // wide

    def load_in(which, own, turn):
        source, target = ((gate_hbm, gate_ref), (up_hbm, up_ref))[which]
        part = (own, slice(None), pl.ds(turn * step, step))
        return pltpu.make_async_copy(source.at[part], target.at[part], in_sem.at[which, own, turn])

    def load_down(own, turn):
        part = (own, slice(None), pl.ds(turn * wide, wide))
        return pltpu.make_async_copy(down_hbm.at[part], down_ref.at[part], down_sem.at[own, turn])

    for own in range(owned):
        for turn in range(turns):
            load_in(0, own, turn).start()
            load_in(1, own, turn).start()
    for turn in range(ends):
        for own in range(owned):
            load_down(own, turn).start()
    rows_ref[:count] = own_ref[...]
    rows_ref[count:] = got_ref[...]
    extra = rows_ref[:, width:].astype(jnp.float32)
    lane = lax.broadcasted_iota(jnp.int32, extra.shape, 1)
    weights = []
    for own in range(owned):
        expert = first_ref[0] + own
        named = (lane == expert) | (lane == expert + experts)
        weights.append(jnp.sum(jnp.where(named, extra, 0.0), axis=1, keepdims=True))
        for turn in range(turns):
            part = pl.ds(turn * step, step)
            x = rows_ref[:, :width]
            load_in(0, own, turn).wait()
            gate = jnp.dot(x, gate_ref[own, :, part], preferred_element_type=jnp.float32)
            load_in(1, own, turn).wait()
            up = jnp.dot(x, up_ref[own, :, part], preferred_element_type=jnp.float32)
            hidden = gate / (1.0 + jnp.exp(-gate)) * up
            hidden_ref[own, :, part] = hidden.astype(jnp.bfloat16)
    for turn in range(ends):
        part = pl.ds(turn * wide, wide)
        total = None
        for own in range(owned):
            load_down(own, turn).wait()
            term = jnp.dot(
                hidden_ref[own], down_ref[own, :, part], preferred_element_type=jnp.float32
            ) * weights[own]
            total = term if total is None else total + term
        total = total.astype(jnp.bfloat16)
        kept_ref[:, part] = total[:count]
        sent_ref[:, part] = total[count:]


def experts_of(own, got, first, experts, expert_gate, expert_up, expert_down):
    count, packed = own.shape
    owned, width, units = expert_gate.shape
    scalars = jnp.stack([first, jnp.int32(experts)])
    vmem = pl.BlockSpec(memory_space=pltpu.VMEM)
    hbm = pl.BlockSpec(memory_space=pltpu.HBM)
    half = jax.ShapeDtypeStruct((count, width), jnp.bfloat16)
    step = min(units, 256)
    wide = 512 if width % 512 == 0 else 128
    return pl.pallas_call(
        experts_kernel,
        out_shape=(half, half),
        in_specs=[pl.BlockSpec(memory_space=pltpu.SMEM), vmem, vmem, hbm, hbm, hbm],
        out_specs=(vmem, vmem),
        scratch_shapes=[
            pltpu.VMEM((2 * count, packed), jnp.bfloat16),
            pltpu.VMEM((owned, 2 * count, units), jnp.bfloat16),
            pltpu.VMEM(expert_gate.shape, jnp.bfloat16),
            pltpu.VMEM(expert_up.shape, jnp.bfloat16),
            pltpu.VMEM(expert_down.shape, jnp.bfloat16),
            pltpu.SemaphoreType.DMA((2, owned, units // step)),
            pltpu.SemaphoreType.DMA((owned, width // wide)),
        ],
        compiler_params=pltpu.CompilerParams(vmem_limit_bytes=VMEM_LIMIT),
        cost_estimate=pl.CostEstimate(
            flops=120 * count * owned * width * units,
            bytes_accessed=6 * owned * width * units,
            transcendentals=2 * count * owned * units,
        ),
        name="experts",
    )(scalars, own, got, expert_gate, expert_up, expert_down)


def attend(queries, new_latent, cache, lengths):
    steps = queries.shape[1]
    ctx = cache.shape[1]
    keys = jnp.concatenate([cache, new_latent], axis=1)
    scores = jnp.einsum("rshl,rkl->rshk", queries, keys, preferred_element_type=jnp.float32) * SCALE
    position = jnp.arange(ctx + steps)
    step_index = jnp.arange(steps)
    in_cache = position[None, :] < lengths[:, None]
    in_new = (position[None, :] >= ctx) & (position[None, :] - ctx <= step_index[:, None])
    allowed = in_cache[:, None, :] | in_new[None, :, :]
    scores = jnp.where(allowed[:, :, None, :], scores, -jnp.inf)
    top = jnp.max(scores, axis=-1, keepdims=True)
    weights = jnp.exp(scores - top)
    weights = (weights / jnp.sum(weights, axis=-1, keepdims=True)).astype(jnp.bfloat16)
    values = keys[:, :, :VDIM]
    return jnp.einsum("rshk,rkv->rshv", weights, values, preferred_element_type=jnp.float32).astype(
        jnp.bfloat16
    )


def body(
    prompt_pages,
    send_page,
    page_table,
    context_len,
    new_latent,
    queries,
    moe_rows,
    routing,
    gate_weights,
    expert_gate,
    expert_up,
    expert_down,
):
    peers = lax.axis_size("dev")
    pages = prompt_pages[0]
    outgoing_slots = send_page[0]
    page_len, width_lat = (pages.shape[1], pages.shape[2])
    capp = outgoing_slots.shape[0] // peers
    picked_pages = pages[jnp.maximum(outgoing_slots, 0)]
    owned = expert_gate.shape[0]
    experts = peers * owned
    rows = routing.shape[1]
    width = moe_rows.shape[2]
    named = routing[0][:, :, None] == jnp.arange(experts)[None, None, :]
    dense = jnp.sum(jnp.where(named, gate_weights[0][:, :, None], 0.0), axis=1)
    high = dense.astype(jnp.bfloat16)
    low = (dense - high.astype(jnp.float32)).astype(jnp.bfloat16)
    extra = jnp.concatenate([high, low], axis=1)
    pad = -extra.shape[1] % 128
    packed = jnp.concatenate([moe_rows[0], jnp.pad(extra, ((0, 0), (0, pad)))], axis=1)
    far, near, last = levels_of(peers, lax.axis_size(("section", "tp")))
    pooled = packed[None]
    for bits in pairs_of(far):
        pooled = jnp.concatenate([pooled] + [exchange(pooled, mask) for mask in masks_of(bits)[1:]], axis=0)
    pooled = pooled.reshape(-1, packed.shape[1])
    pooled = jnp.concatenate([pooled] + [exchange(pooled, mask) for mask in masks_of(near)[1:]], axis=0)
    arrived = lax.all_to_all(
        picked_pages.reshape(peers, capp, page_len, width_lat),
        "dev",
        split_axis=0,
        concat_axis=0,
        tiled=True,
    )
    arrived = arrived.reshape(peers * capp, page_len, width_lat)
    other = masks_of(last)[-1]
    first = lax.axis_index("dev") * owned
    kept, sent = experts_of(
        pooled, exchange(pooled, other), first, experts, expert_gate, expert_up, expert_down
    )
    mixed = kept.astype(jnp.float32) + exchange(sent, other).astype(jnp.float32)
    mixed = mixed.astype(jnp.bfloat16)
    for bits in [near] + pairs_of(far)[::-1]:
        mixed = collect(mixed, bits)

    table = page_table[0]
    requests, most_pages = table.shape
    cache = arrived[jnp.maximum(table, 0)].reshape(requests, most_pages * page_len, width_lat)
    attended = attend(queries[0], new_latent[0], cache, context_len[0])
    return (attended[None], mixed[None])


def solution(mesh):
    rank = ("grp",) + RANK
    return jax.shard_map(
        body,
        mesh=mesh,
        in_specs=(
            P(rank, None, None, None),
            P(rank, None),
            P(rank, None, None),
            P(rank, None),
            P(rank, None, None, None),
            P(rank, None, None, None, None),
            P(rank, None, None),
            P(rank, None, None),
            P(rank, None, None),
            P("dev", None, ("section", "tp")),
            P("dev", None, ("section", "tp")),
            P("dev", ("section", "tp"), None),
        ),
        out_specs=(
            P(rank, None, None, None, None),
            P(rank, None, None),
        ),
        check_vma=False,
    )
```

```python
import functools
import jax
import jax.numpy as jnp
from jax import lax
from jax.experimental import pallas as pl
from jax.experimental.pallas import tpu as pltpu
from jax.sharding import PartitionSpec as P

VDIM = 512
SCALE = 192.0 ** (-0.5)
RANK = ("dev", "section", "tp")
VMEM_LIMIT = 50 * 1024 * 1024


def levels_of(peers, blocks):
    low = blocks.bit_length() - 1
    bits = peers.bit_length() - 1
    far = [low + bit for bit in range(2, bits)]
    near = list(range(low)) + [low + bit for bit in range(1, min(bits, 2))]
    last = [low + bit for bit in range(min(bits, 1))]
    return far, near, last


def masks_of(bits):
    masks = [0]
    for bit in bits:
        masks += [mask | (1 << bit) for mask in masks]
    return masks


def exchange(value, mask):
    count = lax.axis_size(RANK)
    return lax.ppermute(value, RANK, [(at, at ^ mask) for at in range(count)])


def pairs_of(bits):
    return [bits[at : at + 2] for at in range(0, len(bits), 2)]


def collect(value, bits):
    masks = masks_of(bits)
    count = value.shape[0] // len(masks)
    total = value[:count].astype(jnp.float32)
    for turn in range(1, len(masks)):
        sent = value[turn * count : (turn + 1) * count]
        total = total + exchange(sent, masks[turn]).astype(jnp.float32)
    return total.astype(jnp.bfloat16)


def experts_kernel(
    first_ref, own_ref, got_ref, gate_hbm, up_hbm, down_hbm, kept_ref, sent_ref,
    rows_ref, hidden_ref, gate_ref, up_ref, down_ref, in_sem, down_sem,
):
    count = own_ref.shape[0]
    owned, width, units = gate_hbm.shape
    experts = first_ref[1]
    step = min(units, 256)
    wide = 512 if width % 512 == 0 else 128
    turns, ends = units // step, width // wide

    def load_in(which, own, turn):
        source, target = ((gate_hbm, gate_ref), (up_hbm, up_ref))[which]
        part = (own, slice(None), pl.ds(turn * step, step))
        return pltpu.make_async_copy(source.at[part], target.at[part], in_sem.at[which, own, turn])

    def load_down(own, turn):
        part = (own, slice(None), pl.ds(turn * wide, wide))
        return pltpu.make_async_copy(down_hbm.at[part], down_ref.at[part], down_sem.at[own, turn])

    for own in range(owned):
        for turn in range(turns):
            load_in(0, own, turn).start()
            load_in(1, own, turn).start()
    for turn in range(ends):
        for own in range(owned):
            load_down(own, turn).start()
    rows_ref[:count] = own_ref[...]
    rows_ref[count:] = got_ref[...]
    extra = rows_ref[:, width:].astype(jnp.float32)
    lane = lax.broadcasted_iota(jnp.int32, extra.shape, 1)
    weights = []
    for own in range(owned):
        expert = first_ref[0] + own
        named = (lane == expert) | (lane == expert + experts)
        weights.append(jnp.sum(jnp.where(named, extra, 0.0), axis=1, keepdims=True))
        for turn in range(turns):
            part = pl.ds(turn * step, step)
            x = rows_ref[:, :width]
            load_in(0, own, turn).wait()
            gate = jnp.dot(x, gate_ref[own, :, part], preferred_element_type=jnp.float32)
            load_in(1, own, turn).wait()
            up = jnp.dot(x, up_ref[own, :, part], preferred_element_type=jnp.float32)
            hidden = gate / (1.0 + jnp.exp(-gate)) * up
            hidden_ref[own, :, part] = hidden.astype(jnp.bfloat16)
    for turn in range(ends):
        part = pl.ds(turn * wide, wide)
        total = None
        for own in range(owned):
            load_down(own, turn).wait()
            term = jnp.dot(
                hidden_ref[own], down_ref[own, :, part], preferred_element_type=jnp.float32
            ) * weights[own]
            total = term if total is None else total + term
        total = total.astype(jnp.bfloat16)
        kept_ref[:, part] = total[:count]
        sent_ref[:, part] = total[count:]


def experts_of(own, got, first, experts, expert_gate, expert_up, expert_down):
    count, packed = own.shape
    owned, width, units = expert_gate.shape
    scalars = jnp.stack([first, jnp.int32(experts)])
    vmem = pl.BlockSpec(memory_space=pltpu.VMEM)
    hbm = pl.BlockSpec(memory_space=pltpu.HBM)
    half = jax.ShapeDtypeStruct((count, width), jnp.bfloat16)
    step = min(units, 256)
    wide = 512 if width % 512 == 0 else 128
    return pl.pallas_call(
        experts_kernel,
        out_shape=(half, half),
        in_specs=[pl.BlockSpec(memory_space=pltpu.SMEM), vmem, vmem, hbm, hbm, hbm],
        out_specs=(vmem, vmem),
        scratch_shapes=[
            pltpu.VMEM((2 * count, packed), jnp.bfloat16),
            pltpu.VMEM((owned, 2 * count, units), jnp.bfloat16),
            pltpu.VMEM(expert_gate.shape, jnp.bfloat16),
            pltpu.VMEM(expert_up.shape, jnp.bfloat16),
            pltpu.VMEM(expert_down.shape, jnp.bfloat16),
            pltpu.SemaphoreType.DMA((2, owned, units // step)),
            pltpu.SemaphoreType.DMA((owned, width // wide)),
        ],
        compiler_params=pltpu.CompilerParams(vmem_limit_bytes=VMEM_LIMIT),
        cost_estimate=pl.CostEstimate(
            flops=48 * count * owned * width * units,
            bytes_accessed=6 * owned * width * units,
            transcendentals=2 * count * owned * units,
        ),
        name="experts",
    )(scalars, own, got, expert_gate, expert_up, expert_down)


def pick_kernel(capp, me_ref, send_ref, pages_ref, out_ref, sems):
    copies = []
    for at in range(out_ref.shape[0]):
        slot = ((at // capp) ^ me_ref[0]) * capp + at % capp
        page = jnp.maximum(send_ref[slot], 0)
        copies.append(pltpu.make_async_copy(pages_ref.at[page], out_ref.at[at], sems.at[at]))
        copies[-1].start()
    for copy in copies:
        copy.wait()


def pick_pages(pages, outgoing_slots, me, capp):
    slots = outgoing_slots.shape[0]
    smem = pl.BlockSpec(memory_space=pltpu.SMEM)
    return pl.pallas_call(
        functools.partial(pick_kernel, capp),
        out_shape=jax.ShapeDtypeStruct((slots,) + pages.shape[1:], pages.dtype),
        in_specs=[smem, smem, pl.BlockSpec(memory_space=pl.ANY)],
        out_specs=pl.BlockSpec(memory_space=pltpu.VMEM),
        scratch_shapes=[pltpu.SemaphoreType.DMA((slots,))],
        cost_estimate=pl.CostEstimate(flops=0, bytes_accessed=4 * pages[0].size * slots, transcendentals=0),
        name="pick",
    )(me.reshape(1), outgoing_slots, pages)


def attend(queries, new_latent, cache, lengths):
    steps = queries.shape[1]
    ctx = cache.shape[1]
    keys = jnp.concatenate([cache, new_latent], axis=1)
    scores = jnp.einsum("rshl,rkl->rshk", queries, keys, preferred_element_type=jnp.float32) * SCALE
    position = jnp.arange(ctx + steps)
    step_index = jnp.arange(steps)
    in_cache = position[None, :] < lengths[:, None]
    in_new = (position[None, :] >= ctx) & (position[None, :] - ctx <= step_index[:, None])
    allowed = in_cache[:, None, :] | in_new[None, :, :]
    scores = jnp.where(allowed[:, :, None, :], scores, -jnp.inf)
    top = jnp.max(scores, axis=-1, keepdims=True)
    weights = jnp.exp(scores - top)
    weights = (weights / jnp.sum(weights, axis=-1, keepdims=True)).astype(jnp.bfloat16)
    values = keys[:, :, :VDIM]
    return jnp.einsum("rshk,rkv->rshv", weights, values, preferred_element_type=jnp.float32).astype(
        jnp.bfloat16
    )


def body(
    prompt_pages,
    send_page,
    page_table,
    context_len,
    new_latent,
    queries,
    moe_rows,
    routing,
    gate_weights,
    expert_gate,
    expert_up,
    expert_down,
):
    peers = lax.axis_size("dev")
    pages = prompt_pages[0]
    outgoing_slots = send_page[0]
    page_len, width_lat = (pages.shape[1], pages.shape[2])
    capp = outgoing_slots.shape[0] // peers
    me = lax.axis_index("dev")
    sent_pages = pick_pages(pages, outgoing_slots, me, capp)
    owned = expert_gate.shape[0]
    experts = peers * owned
    rows = routing.shape[1]
    width = moe_rows.shape[2]
    named = routing[0][:, :, None] == jnp.arange(experts)[None, None, :]
    dense = jnp.sum(jnp.where(named, gate_weights[0][:, :, None], 0.0), axis=1)
    high = dense.astype(jnp.bfloat16)
    low = (dense - high.astype(jnp.float32)).astype(jnp.bfloat16)
    extra = jnp.concatenate([high, low], axis=1)
    pad = -extra.shape[1] % 128
    packed = jnp.concatenate([moe_rows[0], jnp.pad(extra, ((0, 0), (0, pad)))], axis=1)
    blocks = lax.axis_size(("section", "tp"))
    far, near, last = levels_of(peers, blocks)
    middle = near[-1]
    masks = masks_of(far)
    pooled = packed[None]
    for bits in pairs_of(far):
        pooled = jnp.concatenate([pooled] + [exchange(pooled, mask) for mask in masks_of(bits)[1:]], axis=0)
    pooled, moving = lax.optimization_barrier((pooled, sent_pages))
    moving = moving.reshape(len(masks), 2, 2, -1, width_lat)
    pooled = pooled.reshape(-1, packed.shape[1])
    early = [exchange(moving[turn], masks[turn]) for turn in range(1, len(masks) - 1)]
    pooled = jnp.concatenate([pooled] + [exchange(pooled, mask) for mask in masks_of(near)[1:]], axis=0)
    pooled, early, moving = lax.optimization_barrier((pooled, early, moving))
    crossed = exchange(jnp.stack([moving[0, 1]] + [part[1] for part in early]), 1 << middle)
    late = [exchange(moving[-1, 0], masks[-1]), exchange(moving[-1, 1], masks[-1] | 1 << middle)]
    other = masks_of(last)[-1]
    first = me * owned
    kept, sent = experts_of(
        pooled, exchange(pooled, other), first, experts, expert_gate, expert_up, expert_down
    )
    kept, sent, crossed, late = lax.optimization_barrier((kept, sent, crossed, late))
    mixed = kept.astype(jnp.float32) + exchange(sent, other).astype(jnp.float32)
    mixed, crossed, late = lax.optimization_barrier((mixed.astype(jnp.bfloat16), crossed, late))
    straight = jnp.stack([moving[0, 0]] + [part[0] for part in early] + [late[0]])
    crossed = jnp.concatenate([crossed, late[1][None]])
    away = exchange(jnp.stack([straight[:, 1], crossed[:, 1]], axis=1), other)
    moving = jnp.stack([jnp.stack([straight[:, 0], crossed[:, 0]], axis=1), away], axis=2)
    mixed = collect(mixed, near)
    mixed, moving = lax.optimization_barrier((mixed, moving))
    for bits in pairs_of(far)[::-1]:
        mixed = collect(mixed, bits)
    arrived = moving.reshape(peers * capp, page_len, width_lat)

    table = page_table[0]
    requests, most_pages = table.shape
    slots = jnp.maximum(table, 0)
    slots = ((slots // capp) ^ me) * capp + slots % capp
    cache = arrived[slots].reshape(requests, most_pages * page_len, width_lat)
    attended = attend(queries[0], new_latent[0], cache, context_len[0])
    return (attended[None], mixed[None])


def solution(mesh):
    rank = ("grp",) + RANK
    return jax.shard_map(
        body,
        mesh=mesh,
        in_specs=(
            P(rank, None, None, None),
            P(rank, None),
            P(rank, None, None),
            P(rank, None),
            P(rank, None, None, None),
            P(rank, None, None, None, None),
            P(rank, None, None),
            P(rank, None, None),
            P(rank, None, None),
            P("dev", None, ("section", "tp")),
            P("dev", None, ("section", "tp")),
            P("dev", ("section", "tp"), None),
        ),
        out_specs=(
            P(rank, None, None, None, None),
            P(rank, None, None),
        ),
        check_vma=False,
    )
```

```python
import jax
import jax.numpy as jnp
from jax import lax
from jax.experimental import pallas as pl
from jax.experimental.pallas import tpu as pltpu
from jax.sharding import PartitionSpec as P

VDIM = 512
SCALE = 192.0 ** (-0.5)
RANK = ("dev", "section", "tp")
VMEM_LIMIT = 50 * 1024 * 1024


def levels_of(peers, blocks):
    low = blocks.bit_length() - 1
    bits = peers.bit_length() - 1
    far = [low + bit for bit in range(2, bits)]
    near = list(range(low)) + [low + bit for bit in range(1, min(bits, 2))]
    last = [low + bit for bit in range(min(bits, 1))]
    return far, near, last


def masks_of(bits):
    masks = [0]
    for bit in bits:
        masks += [mask | (1 << bit) for mask in masks]
    return masks


def exchange(value, mask):
    count = lax.axis_size(RANK)
    return lax.ppermute(value, RANK, [(at, at ^ mask) for at in range(count)])


def pairs_of(bits):
    return [bits[at : at + 2] for at in range(0, len(bits), 2)]


def collect(value, bits):
    masks = masks_of(bits)
    count = value.shape[0] // len(masks)
    total = value[:count].astype(jnp.float32)
    for turn in range(1, len(masks)):
        sent = value[turn * count : (turn + 1) * count]
        total = total + exchange(sent, masks[turn]).astype(jnp.float32)
    return total.astype(jnp.bfloat16)


def experts_kernel(
    first_ref, own_ref, got_ref, gate_hbm, up_hbm, down_hbm, kept_ref, sent_ref,
    rows_ref, hidden_ref, gate_ref, up_ref, down_ref, in_sem, down_sem,
):
    count = own_ref.shape[0]
    owned, width, units = gate_hbm.shape
    experts = first_ref[1]
    step = min(units, 256)
    wide = 512 if width % 512 == 0 else 128
    turns, ends = units // step, width // wide

    def load_in(which, own, turn):
        source, target = ((gate_hbm, gate_ref), (up_hbm, up_ref))[which]
        part = (own, slice(None), pl.ds(turn * step, step))
        return pltpu.make_async_copy(source.at[part], target.at[part], in_sem.at[which, own, turn])

    def load_down(own, turn):
        part = (own, slice(None), pl.ds(turn * wide, wide))
        return pltpu.make_async_copy(down_hbm.at[part], down_ref.at[part], down_sem.at[own, turn])

    for own in range(owned):
        for turn in range(turns):
            load_in(0, own, turn).start()
            load_in(1, own, turn).start()
    for turn in range(ends):
        for own in range(owned):
            load_down(own, turn).start()
    rows_ref[:count] = own_ref[...]
    rows_ref[count:] = got_ref[...]
    extra = rows_ref[:, width:].astype(jnp.float32)
    lane = lax.broadcasted_iota(jnp.int32, extra.shape, 1)
    weights = []
    for own in range(owned):
        expert = first_ref[0] + own
        named = (lane == expert) | (lane == expert + experts)
        weights.append(jnp.sum(jnp.where(named, extra, 0.0), axis=1, keepdims=True))
        for turn in range(turns):
            part = pl.ds(turn * step, step)
            x = rows_ref[:, :width]
            load_in(0, own, turn).wait()
            gate = jnp.dot(x, gate_ref[own, :, part], preferred_element_type=jnp.float32)
            load_in(1, own, turn).wait()
            up = jnp.dot(x, up_ref[own, :, part], preferred_element_type=jnp.float32)
            hidden = gate / (1.0 + jnp.exp(-gate)) * up
            hidden_ref[own, :, part] = hidden.astype(jnp.bfloat16)
    for turn in range(ends):
        part = pl.ds(turn * wide, wide)
        total = None
        for own in range(owned):
            load_down(own, turn).wait()
            term = jnp.dot(
                hidden_ref[own], down_ref[own, :, part], preferred_element_type=jnp.float32
            ) * weights[own]
            total = term if total is None else total + term
        total = total.astype(jnp.bfloat16)
        kept_ref[:, part] = total[:count]
        sent_ref[:, part] = total[count:]


def experts_of(own, got, first, experts, expert_gate, expert_up, expert_down):
    count, packed = own.shape
    owned, width, units = expert_gate.shape
    scalars = jnp.stack([first, jnp.int32(experts)])
    vmem = pl.BlockSpec(memory_space=pltpu.VMEM)
    hbm = pl.BlockSpec(memory_space=pltpu.HBM)
    half = jax.ShapeDtypeStruct((count, width), jnp.bfloat16)
    step = min(units, 256)
    wide = 512 if width % 512 == 0 else 128
    return pl.pallas_call(
        experts_kernel,
        out_shape=(half, half),
        in_specs=[pl.BlockSpec(memory_space=pltpu.SMEM), vmem, vmem, hbm, hbm, hbm],
        out_specs=(vmem, vmem),
        scratch_shapes=[
            pltpu.VMEM((2 * count, packed), jnp.bfloat16),
            pltpu.VMEM((owned, 2 * count, units), jnp.bfloat16),
            pltpu.VMEM(expert_gate.shape, jnp.bfloat16),
            pltpu.VMEM(expert_up.shape, jnp.bfloat16),
            pltpu.VMEM(expert_down.shape, jnp.bfloat16),
            pltpu.SemaphoreType.DMA((2, owned, units // step)),
            pltpu.SemaphoreType.DMA((owned, width // wide)),
        ],
        compiler_params=pltpu.CompilerParams(vmem_limit_bytes=VMEM_LIMIT),
        cost_estimate=pl.CostEstimate(
            flops=120 * count * owned * width * units,
            bytes_accessed=6 * owned * width * units,
            transcendentals=2 * count * owned * units,
        ),
        name="experts",
    )(scalars, own, got, expert_gate, expert_up, expert_down)


def attend(queries, new_latent, cache, lengths):
    steps = queries.shape[1]
    ctx = cache.shape[1]
    keys = jnp.concatenate([cache, new_latent], axis=1)
    scores = jnp.einsum("rshl,rkl->rshk", queries, keys, preferred_element_type=jnp.float32) * SCALE
    position = jnp.arange(ctx + steps)
    step_index = jnp.arange(steps)
    in_cache = position[None, :] < lengths[:, None]
    in_new = (position[None, :] >= ctx) & (position[None, :] - ctx <= step_index[:, None])
    allowed = in_cache[:, None, :] | in_new[None, :, :]
    scores = jnp.where(allowed[:, :, None, :], scores, -jnp.inf)
    top = jnp.max(scores, axis=-1, keepdims=True)
    weights = jnp.exp(scores - top)
    weights = (weights / jnp.sum(weights, axis=-1, keepdims=True)).astype(jnp.bfloat16)
    values = keys[:, :, :VDIM]
    return jnp.einsum("rshk,rkv->rshv", weights, values, preferred_element_type=jnp.float32).astype(
        jnp.bfloat16
    )


def body(
    prompt_pages,
    send_page,
    page_table,
    context_len,
    new_latent,
    queries,
    moe_rows,
    routing,
    gate_weights,
    expert_gate,
    expert_up,
    expert_down,
):
    peers = lax.axis_size("dev")
    pages = prompt_pages[0]
    outgoing_slots = send_page[0]
    page_len, width_lat = (pages.shape[1], pages.shape[2])
    capp = outgoing_slots.shape[0] // peers
    picked_pages = pages[jnp.maximum(outgoing_slots, 0)]
    arrived = lax.all_to_all(
        picked_pages.reshape(peers, capp, page_len, width_lat),
        "dev",
        split_axis=0,
        concat_axis=0,
        tiled=True,
    )
    arrived = arrived.reshape(peers * capp, page_len, width_lat)

    owned = expert_gate.shape[0]
    experts = peers * owned
    rows = routing.shape[1]
    width = moe_rows.shape[2]
    named = routing[0][:, :, None] == jnp.arange(experts)[None, None, :]
    dense = jnp.sum(jnp.where(named, gate_weights[0][:, :, None], 0.0), axis=1)
    high = dense.astype(jnp.bfloat16)
    low = (dense - high.astype(jnp.float32)).astype(jnp.bfloat16)
    extra = jnp.concatenate([high, low], axis=1)
    pad = -extra.shape[1] % 128
    packed = jnp.concatenate([moe_rows[0], jnp.pad(extra, ((0, 0), (0, pad)))], axis=1)
    far, near, last = levels_of(peers, lax.axis_size(("section", "tp")))
    pooled = packed
    for bits in pairs_of(far):
        pooled = jnp.concatenate([pooled] + [exchange(pooled, mask) for mask in masks_of(bits)[1:]], axis=0)
    pooled = jnp.concatenate([pooled] + [exchange(pooled, mask) for mask in masks_of(near)[1:]], axis=0)
    other = masks_of(last)[-1]
    first = lax.axis_index("dev") * owned
    kept, sent = experts_of(
        pooled, exchange(pooled, other), first, experts, expert_gate, expert_up, expert_down
    )
    mixed = kept.astype(jnp.float32) + exchange(sent, other).astype(jnp.float32)
    mixed = mixed.astype(jnp.bfloat16)
    for bits in [near] + pairs_of(far)[::-1]:
        mixed = collect(mixed, bits)

    table = page_table[0]
    requests, most_pages = table.shape
    cache = arrived[jnp.maximum(table, 0)].reshape(requests, most_pages * page_len, width_lat)
    attended = attend(queries[0], new_latent[0], cache, context_len[0])
    return (attended[None], mixed[None])


def solution(mesh):
    rank = ("grp",) + RANK
    return jax.shard_map(
        body,
        mesh=mesh,
        in_specs=(
            P(rank, None, None, None),
            P(rank, None),
            P(rank, None, None),
            P(rank, None),
            P(rank, None, None, None),
            P(rank, None, None, None, None),
            P(rank, None, None),
            P(rank, None, None),
            P(rank, None, None),
            P("dev", None, ("section", "tp")),
            P("dev", None, ("section", "tp")),
            P("dev", ("section", "tp"), None),
        ),
        out_specs=(
            P(rank, None, None, None, None),
            P(rank, None, None),
        ),
        check_vma=False,
    )
```

```python
import jax
import jax.numpy as jnp
from jax import lax
from jax.experimental import pallas as pl
from jax.experimental.pallas import tpu as pltpu
from jax.sharding import PartitionSpec as P

VDIM = 512
SCALE = 192.0 ** (-0.5)
RANK = ("dev", "section", "tp")
VMEM_LIMIT = 50 * 1024 * 1024


def levels_of(peers, blocks):
    low = blocks.bit_length() - 1
    bits = peers.bit_length() - 1
    far = [low + bit for bit in range(2, bits)]
    near = list(range(low)) + [low + bit for bit in range(1, min(bits, 2))]
    last = [low + bit for bit in range(min(bits, 1))]
    return far, near, last


def masks_of(bits):
    masks = [0]
    for bit in bits:
        masks += [mask | (1 << bit) for mask in masks]
    return masks


def exchange(value, mask):
    count = lax.axis_size(RANK)
    return lax.ppermute(value, RANK, [(at, at ^ mask) for at in range(count)])


def pairs_of(bits):
    return [bits[at : at + 2] for at in range(0, len(bits), 2)]


def collect(value, bits):
    masks = masks_of(bits)
    count = value.shape[0] // len(masks)
    total = value[:count].astype(jnp.float32)
    for turn in range(1, len(masks)):
        sent = value[turn * count : (turn + 1) * count]
        total = total + exchange(sent, masks[turn]).astype(jnp.float32)
    return total.astype(jnp.bfloat16)


def experts_kernel(
    first_ref, own_ref, got_ref, gate_hbm, up_hbm, down_hbm, kept_ref, sent_ref,
    rows_ref, hidden_ref, gate_ref, up_ref, down_ref, in_sem, down_sem,
):
    count = own_ref.shape[0]
    owned, width, units = gate_hbm.shape
    experts = first_ref[1]
    step = min(units, 256)
    wide = 512 if width % 512 == 0 else 128
    turns, ends = units // step, width // wide

    def load_in(which, own, turn):
        source, target = ((gate_hbm, gate_ref), (up_hbm, up_ref))[which]
        part = (own, slice(None), pl.ds(turn * step, step))
        return pltpu.make_async_copy(source.at[part], target.at[part], in_sem.at[which, own, turn])

    def load_down(own, turn):
        part = (own, slice(None), pl.ds(turn * wide, wide))
        return pltpu.make_async_copy(down_hbm.at[part], down_ref.at[part], down_sem.at[own, turn])

    for own in range(owned):
        for turn in range(turns):
            load_in(0, own, turn).start()
            load_in(1, own, turn).start()
    for turn in range(ends):
        for own in range(owned):
            load_down(own, turn).start()
    rows_ref[:count] = own_ref[...]
    rows_ref[count:] = got_ref[...]
    extra = rows_ref[:, width:].astype(jnp.float32)
    lane = lax.broadcasted_iota(jnp.int32, extra.shape, 1)
    weights = []
    for own in range(owned):
        expert = first_ref[0] + own
        named = (lane == expert) | (lane == expert + experts)
        weights.append(jnp.sum(jnp.where(named, extra, 0.0), axis=1, keepdims=True))
        for turn in range(turns):
            part = pl.ds(turn * step, step)
            x = rows_ref[:, :width]
            load_in(0, own, turn).wait()
            gate = jnp.dot(x, gate_ref[own, :, part], preferred_element_type=jnp.float32)
            load_in(1, own, turn).wait()
            up = jnp.dot(x, up_ref[own, :, part], preferred_element_type=jnp.float32)
            hidden = gate / (1.0 + jnp.exp(-gate)) * up
            hidden_ref[own, :, part] = hidden.astype(jnp.bfloat16)
    for turn in range(ends):
        part = pl.ds(turn * wide, wide)
        total = None
        for own in range(owned):
            load_down(own, turn).wait()
            term = jnp.dot(
                hidden_ref[own], down_ref[own, :, part], preferred_element_type=jnp.float32
            ) * weights[own]
            total = term if total is None else total + term
        total = total.astype(jnp.bfloat16)
        kept_ref[:, part] = total[:count]
        sent_ref[:, part] = total[count:]


def experts_of(own, got, first, experts, expert_gate, expert_up, expert_down):
    count, packed = own.shape
    owned, width, units = expert_gate.shape
    scalars = jnp.stack([first, jnp.int32(experts)])
    vmem = pl.BlockSpec(memory_space=pltpu.VMEM)
    hbm = pl.BlockSpec(memory_space=pltpu.HBM)
    half = jax.ShapeDtypeStruct((count, width), jnp.bfloat16)
    step = min(units, 256)
    wide = 512 if width % 512 == 0 else 128
    return pl.pallas_call(
        experts_kernel,
        out_shape=(half, half),
        in_specs=[pl.BlockSpec(memory_space=pltpu.SMEM), vmem, vmem, hbm, hbm, hbm],
        out_specs=(vmem, vmem),
        scratch_shapes=[
            pltpu.VMEM((2 * count, packed), jnp.bfloat16),
            pltpu.VMEM((owned, 2 * count, units), jnp.bfloat16),
            pltpu.VMEM(expert_gate.shape, jnp.bfloat16),
            pltpu.VMEM(expert_up.shape, jnp.bfloat16),
            pltpu.VMEM(expert_down.shape, jnp.bfloat16),
            pltpu.SemaphoreType.DMA((2, owned, units // step)),
            pltpu.SemaphoreType.DMA((owned, width // wide)),
        ],
        compiler_params=pltpu.CompilerParams(vmem_limit_bytes=VMEM_LIMIT),
        cost_estimate=pl.CostEstimate(
            flops=120 * count * owned * width * units,
            bytes_accessed=6 * owned * width * units,
            transcendentals=2 * count * owned * units,
        ),
        name="experts",
    )(scalars, own, got, expert_gate, expert_up, expert_down)


def attend(queries, new_latent, cache, lengths):
    steps = queries.shape[1]
    ctx = cache.shape[1]
    keys = jnp.concatenate([cache, new_latent], axis=1)
    scores = jnp.einsum("rshl,rkl->rshk", queries, keys, preferred_element_type=jnp.float32) * SCALE
    position = jnp.arange(ctx + steps)
    step_index = jnp.arange(steps)
    in_cache = position[None, :] < lengths[:, None]
    in_new = (position[None, :] >= ctx) & (position[None, :] - ctx <= step_index[:, None])
    allowed = in_cache[:, None, :] | in_new[None, :, :]
    scores = jnp.where(allowed[:, :, None, :], scores, -jnp.inf)
    top = jnp.max(scores, axis=-1, keepdims=True)
    weights = jnp.exp(scores - top)
    weights = (weights / jnp.sum(weights, axis=-1, keepdims=True)).astype(jnp.bfloat16)
    values = keys[:, :, :VDIM]
    return jnp.einsum("rshk,rkv->rshv", weights, values, preferred_element_type=jnp.float32).astype(
        jnp.bfloat16
    )


def body(
    prompt_pages,
    send_page,
    page_table,
    context_len,
    new_latent,
    queries,
    moe_rows,
    routing,
    gate_weights,
    expert_gate,
    expert_up,
    expert_down,
):
    peers = lax.axis_size("dev")
    pages = prompt_pages[0]
    outgoing_slots = send_page[0]
    page_len, width_lat = (pages.shape[1], pages.shape[2])
    capp = outgoing_slots.shape[0] // peers
    picked_pages = pages[jnp.maximum(outgoing_slots, 0)]
    arrived = lax.all_to_all(
        picked_pages.reshape(peers, capp, page_len, width_lat),
        "dev",
        split_axis=0,
        concat_axis=0,
        tiled=True,
    )
    arrived = arrived.reshape(peers * capp, page_len, width_lat)

    owned = expert_gate.shape[0]
    experts = peers * owned
    rows = routing.shape[1]
    width = moe_rows.shape[2]
    named = routing[0][:, :, None] == jnp.arange(experts)[None, None, :]
    dense = jnp.sum(jnp.where(named, gate_weights[0][:, :, None], 0.0), axis=1)
    high = dense.astype(jnp.bfloat16)
    low = (dense - high.astype(jnp.float32)).astype(jnp.bfloat16)
    extra = jnp.concatenate([high, low], axis=1)
    pad = -extra.shape[1] % 128
    packed = jnp.concatenate([moe_rows[0], jnp.pad(extra, ((0, 0), (0, pad)))], axis=1)
    far, near, last = levels_of(peers, lax.axis_size(("section", "tp")))
    pooled = packed
    for bits in pairs_of(far):
        pooled = jnp.concatenate([pooled] + [exchange(pooled, mask) for mask in masks_of(bits)[1:]], axis=0)
    pooled = jnp.concatenate([pooled] + [exchange(pooled, mask) for mask in masks_of(near)[1:]], axis=0)
    other = masks_of(last)[-1]
    first = lax.axis_index("dev") * owned
    kept, sent = experts_of(
        pooled, exchange(pooled, other), first, experts, expert_gate, expert_up, expert_down
    )
    mixed = kept.astype(jnp.float32) + exchange(sent, other).astype(jnp.float32)
    mixed = mixed.astype(jnp.bfloat16)
    mixed = collect(mixed, near)
    mixed, arrived = lax.optimization_barrier((mixed, arrived))
    for bits in pairs_of(far)[::-1]:
        mixed = collect(mixed, bits)

    table = page_table[0]
    requests, most_pages = table.shape
    cache = arrived[jnp.maximum(table, 0)].reshape(requests, most_pages * page_len, width_lat)
    attended = attend(queries[0], new_latent[0], cache, context_len[0])
    return (attended[None], mixed[None])


def solution(mesh):
    rank = ("grp",) + RANK
    return jax.shard_map(
        body,
        mesh=mesh,
        in_specs=(
            P(rank, None, None, None),
            P(rank, None),
            P(rank, None, None),
            P(rank, None),
            P(rank, None, None, None),
            P(rank, None, None, None, None),
            P(rank, None, None),
            P(rank, None, None),
            P(rank, None, None),
            P("dev", None, ("section", "tp")),
            P("dev", None, ("section", "tp")),
            P("dev", ("section", "tp"), None),
        ),
        out_specs=(
            P(rank, None, None, None, None),
            P(rank, None, None),
        ),
        check_vma=False,
    )
```

```python
import jax
import jax.numpy as jnp
from jax import lax
from jax.experimental import pallas as pl
from jax.experimental.pallas import tpu as pltpu
from jax.sharding import PartitionSpec as P

VDIM = 512
SCALE = 192.0 ** (-0.5)
RANK = ("dev", "section", "tp")
VMEM_LIMIT = 50 * 1024 * 1024


def levels_of(peers, blocks):
    low = blocks.bit_length() - 1
    bits = peers.bit_length() - 1
    far = [low + bit for bit in range(2, bits)]
    near = list(range(low)) + [low + bit for bit in range(1, min(bits, 2))]
    last = [low + bit for bit in range(min(bits, 1))]
    return far, near, last


def masks_of(bits):
    masks = [0]
    for bit in bits:
        masks += [mask | (1 << bit) for mask in masks]
    return masks


def exchange(value, mask):
    count = lax.axis_size(RANK)
    return lax.ppermute(value, RANK, [(at, at ^ mask) for at in range(count)])


def pairs_of(bits):
    return [bits[at : at + 2] for at in range(0, len(bits), 2)]


def collect(value, bits):
    masks = masks_of(bits)
    count = value.shape[0] // len(masks)
    total = value[:count].astype(jnp.float32)
    for turn in range(1, len(masks)):
        sent = value[turn * count : (turn + 1) * count]
        total = total + exchange(sent, masks[turn]).astype(jnp.float32)
    return total.astype(jnp.bfloat16)


def experts_kernel(
    first_ref, own_ref, got_ref, gate_hbm, up_hbm, down_hbm, kept_ref, sent_ref,
    rows_ref, hidden_ref, gate_ref, up_ref, down_ref, in_sem, down_sem,
):
    count = own_ref.shape[0]
    owned, width, units = gate_hbm.shape
    experts = first_ref[1]
    step = min(units, 256)
    wide = 512 if width % 512 == 0 else 128
    turns, ends = units // step, width // wide

    def load_in(which, own, turn):
        source, target = ((gate_hbm, gate_ref), (up_hbm, up_ref))[which]
        part = (own, slice(None), pl.ds(turn * step, step))
        return pltpu.make_async_copy(source.at[part], target.at[part], in_sem.at[which, own, turn])

    def load_down(own, turn):
        part = (own, slice(None), pl.ds(turn * wide, wide))
        return pltpu.make_async_copy(down_hbm.at[part], down_ref.at[part], down_sem.at[own, turn])

    order = [(own, turn) for own in range(owned) for turn in range(turns)]

    def load_next(at):
        if at < len(order):
            load_in(0, *order[at]).start()
            load_in(1, *order[at]).start()
        elif at == len(order):
            for turn in range(ends):
                for own in range(owned):
                    load_down(own, turn).start()

    load_next(0)
    rows_ref[:count] = own_ref[...]
    rows_ref[count:] = got_ref[...]
    extra = rows_ref[:, width:].astype(jnp.float32)
    lane = lax.broadcasted_iota(jnp.int32, extra.shape, 1)
    weights = []
    for own in range(owned):
        expert = first_ref[0] + own
        named = (lane == expert) | (lane == expert + experts)
        weights.append(jnp.sum(jnp.where(named, extra, 0.0), axis=1, keepdims=True))
        for turn in range(turns):
            part = pl.ds(turn * step, step)
            x = rows_ref[:, :width]
            load_in(0, own, turn).wait()
            load_next(order.index((own, turn)) + 1)
            gate = jnp.dot(x, gate_ref[own, :, part], preferred_element_type=jnp.float32)
            load_in(1, own, turn).wait()
            up = jnp.dot(x, up_ref[own, :, part], preferred_element_type=jnp.float32)
            hidden = gate / (1.0 + jnp.exp(-gate)) * up
            hidden_ref[own, :, part] = hidden.astype(jnp.bfloat16)
    for turn in range(ends):
        part = pl.ds(turn * wide, wide)
        total = None
        for own in range(owned):
            load_down(own, turn).wait()
            term = jnp.dot(
                hidden_ref[own], down_ref[own, :, part], preferred_element_type=jnp.float32
            ) * weights[own]
            total = term if total is None else total + term
        total = total.astype(jnp.bfloat16)
        kept_ref[:, part] = total[:count]
        sent_ref[:, part] = total[count:]


def experts_of(own, got, first, experts, expert_gate, expert_up, expert_down):
    count, packed = own.shape
    owned, width, units = expert_gate.shape
    scalars = jnp.stack([first, jnp.int32(experts)])
    vmem = pl.BlockSpec(memory_space=pltpu.VMEM)
    hbm = pl.BlockSpec(memory_space=pltpu.HBM)
    half = jax.ShapeDtypeStruct((count, width), jnp.bfloat16)
    step = min(units, 256)
    wide = 512 if width % 512 == 0 else 128
    return pl.pallas_call(
        experts_kernel,
        out_shape=(half, half),
        in_specs=[pl.BlockSpec(memory_space=pltpu.SMEM), vmem, vmem, hbm, hbm, hbm],
        out_specs=(vmem, vmem),
        scratch_shapes=[
            pltpu.VMEM((2 * count, packed), jnp.bfloat16),
            pltpu.VMEM((owned, 2 * count, units), jnp.bfloat16),
            pltpu.VMEM(expert_gate.shape, jnp.bfloat16),
            pltpu.VMEM(expert_up.shape, jnp.bfloat16),
            pltpu.VMEM(expert_down.shape, jnp.bfloat16),
            pltpu.SemaphoreType.DMA((2, owned, units // step)),
            pltpu.SemaphoreType.DMA((owned, width // wide)),
        ],
        compiler_params=pltpu.CompilerParams(vmem_limit_bytes=VMEM_LIMIT),
        cost_estimate=pl.CostEstimate(
            flops=120 * count * owned * width * units,
            bytes_accessed=6 * owned * width * units,
            transcendentals=2 * count * owned * units,
        ),
        name="experts",
    )(scalars, own, got, expert_gate, expert_up, expert_down)


def attend(queries, new_latent, cache, lengths):
    steps = queries.shape[1]
    ctx = cache.shape[1]
    keys = jnp.concatenate([cache, new_latent], axis=1)
    scores = jnp.einsum("rshl,rkl->rshk", queries, keys, preferred_element_type=jnp.float32) * SCALE
    position = jnp.arange(ctx + steps)
    step_index = jnp.arange(steps)
    in_cache = position[None, :] < lengths[:, None]
    in_new = (position[None, :] >= ctx) & (position[None, :] - ctx <= step_index[:, None])
    allowed = in_cache[:, None, :] | in_new[None, :, :]
    scores = jnp.where(allowed[:, :, None, :], scores, -jnp.inf)
    top = jnp.max(scores, axis=-1, keepdims=True)
    weights = jnp.exp(scores - top)
    weights = (weights / jnp.sum(weights, axis=-1, keepdims=True)).astype(jnp.bfloat16)
    values = keys[:, :, :VDIM]
    return jnp.einsum("rshk,rkv->rshv", weights, values, preferred_element_type=jnp.float32).astype(
        jnp.bfloat16
    )


def body(
    prompt_pages,
    send_page,
    page_table,
    context_len,
    new_latent,
    queries,
    moe_rows,
    routing,
    gate_weights,
    expert_gate,
    expert_up,
    expert_down,
):
    peers = lax.axis_size("dev")
    pages = prompt_pages[0]
    outgoing_slots = send_page[0]
    page_len, width_lat = (pages.shape[1], pages.shape[2])
    capp = outgoing_slots.shape[0] // peers
    picked_pages = pages[jnp.maximum(outgoing_slots, 0)]
    arrived = lax.all_to_all(
        picked_pages.reshape(peers, capp, page_len, width_lat),
        "dev",
        split_axis=0,
        concat_axis=0,
        tiled=True,
    )
    arrived = arrived.reshape(peers * capp, page_len, width_lat)

    owned = expert_gate.shape[0]
    experts = peers * owned
    rows = routing.shape[1]
    width = moe_rows.shape[2]
    named = routing[0][:, :, None] == jnp.arange(experts)[None, None, :]
    dense = jnp.sum(jnp.where(named, gate_weights[0][:, :, None], 0.0), axis=1)
    high = dense.astype(jnp.bfloat16)
    low = (dense - high.astype(jnp.float32)).astype(jnp.bfloat16)
    extra = jnp.concatenate([high, low], axis=1)
    pad = -extra.shape[1] % 128
    packed = jnp.concatenate([moe_rows[0], jnp.pad(extra, ((0, 0), (0, pad)))], axis=1)
    far, near, last = levels_of(peers, lax.axis_size(("section", "tp")))
    pooled = packed[None]
    for bits in pairs_of(far):
        pooled = jnp.concatenate([pooled] + [exchange(pooled, mask) for mask in masks_of(bits)[1:]], axis=0)
    pooled = pooled.reshape(-1, packed.shape[1])
    pooled = jnp.concatenate([pooled] + [exchange(pooled, mask) for mask in masks_of(near)[1:]], axis=0)
    other = masks_of(last)[-1]
    first = lax.axis_index("dev") * owned
    kept, sent = experts_of(
        pooled, exchange(pooled, other), first, experts, expert_gate, expert_up, expert_down
    )
    mixed = kept.astype(jnp.float32) + exchange(sent, other).astype(jnp.float32)
    mixed = mixed.astype(jnp.bfloat16)
    mixed = collect(mixed, near)
    mixed, arrived = lax.optimization_barrier((mixed, arrived))
    for bits in pairs_of(far)[::-1]:
        mixed = collect(mixed, bits)

    table = page_table[0]
    requests, most_pages = table.shape
    cache = arrived[jnp.maximum(table, 0)].reshape(requests, most_pages * page_len, width_lat)
    attended = attend(queries[0], new_latent[0], cache, context_len[0])
    return (attended[None], mixed[None])


def solution(mesh):
    rank = ("grp",) + RANK
    return jax.shard_map(
        body,
        mesh=mesh,
        in_specs=(
            P(rank, None, None, None),
            P(rank, None),
            P(rank, None, None),
            P(rank, None),
            P(rank, None, None, None),
            P(rank, None, None, None, None),
            P(rank, None, None),
            P(rank, None, None),
            P(rank, None, None),
            P("dev", None, ("section", "tp")),
            P("dev", None, ("section", "tp")),
            P("dev", ("section", "tp"), None),
        ),
        out_specs=(
            P(rank, None, None, None, None),
            P(rank, None, None),
        ),
        check_vma=False,
    )
```

```python
import jax
import jax.numpy as jnp
from jax import lax
from jax.experimental import pallas as pl
from jax.experimental.pallas import tpu as pltpu
from jax.sharding import PartitionSpec as P

VDIM = 512
SCALE = 192.0 ** (-0.5)
RANK = ("dev", "section", "tp")
VMEM_LIMIT = 50 * 1024 * 1024


def levels_of(peers, blocks):
    low = blocks.bit_length() - 1
    bits = peers.bit_length() - 1
    far = [low + bit for bit in range(2, bits)]
    near = list(range(low)) + [low + bit for bit in range(1, min(bits, 2))]
    last = [low + bit for bit in range(min(bits, 1))]
    return far, near, last


def masks_of(bits):
    masks = [0]
    for bit in bits:
        masks += [mask | (1 << bit) for mask in masks]
    return masks


def exchange(value, mask):
    count = lax.axis_size(RANK)
    return lax.ppermute(value, RANK, [(at, at ^ mask) for at in range(count)])


def pairs_of(bits):
    return [bits[at : at + 2] for at in range(0, len(bits), 2)]


def collect(value, bits):
    masks = masks_of(bits)
    count = value.shape[0] // len(masks)
    total = value[:count].astype(jnp.float32)
    for turn in range(1, len(masks)):
        sent = value[turn * count : (turn + 1) * count]
        total = total + exchange(sent, masks[turn]).astype(jnp.float32)
    return total.astype(jnp.bfloat16)


def experts_kernel(
    first_ref, own_ref, got_ref, gate_hbm, up_hbm, down_hbm, kept_ref, sent_ref,
    rows_ref, hidden_ref, gate_ref, up_ref, down_ref, in_sem, down_sem,
):
    count = own_ref.shape[0]
    owned, width, units = gate_hbm.shape
    experts = first_ref[1]
    step = min(units, 256)
    wide = 512 if width % 512 == 0 else 128
    turns, ends = units // step, width // wide

    def load_in(which, own, turn):
        source, target = ((gate_hbm, gate_ref), (up_hbm, up_ref))[which]
        part = (own, slice(None), pl.ds(turn * step, step))
        return pltpu.make_async_copy(source.at[part], target.at[part], in_sem.at[which, own, turn])

    def load_down(own, turn):
        part = (own, slice(None), pl.ds(turn * wide, wide))
        return pltpu.make_async_copy(down_hbm.at[part], down_ref.at[part], down_sem.at[own, turn])

    order = [(own, turn) for own in range(owned) for turn in range(turns)]

    def load_next(at):
        if at < len(order):
            load_in(0, *order[at]).start()
            load_in(1, *order[at]).start()
        elif at == len(order):
            for turn in range(ends):
                for own in range(owned):
                    load_down(own, turn).start()

    load_next(0)
    rows_ref[:count] = own_ref[...]
    rows_ref[count:] = got_ref[...]
    extra = rows_ref[:, width:].astype(jnp.float32)
    lane = lax.broadcasted_iota(jnp.int32, extra.shape, 1)
    weights = []
    for own in range(owned):
        expert = first_ref[0] + own
        named = (lane == expert) | (lane == expert + experts)
        weights.append(jnp.sum(jnp.where(named, extra, 0.0), axis=1, keepdims=True))
        for turn in range(turns):
            part = pl.ds(turn * step, step)
            x = rows_ref[:, :width]
            load_in(0, own, turn).wait()
            load_next(order.index((own, turn)) + 1)
            gate = jnp.dot(x, gate_ref[own, :, part], preferred_element_type=jnp.float32)
            load_in(1, own, turn).wait()
            up = jnp.dot(x, up_ref[own, :, part], preferred_element_type=jnp.float32)
            hidden = gate / (1.0 + jnp.exp(-gate)) * up
            hidden_ref[own, :, part] = hidden.astype(jnp.bfloat16)
    for turn in range(ends):
        part = pl.ds(turn * wide, wide)
        total = None
        for own in range(owned):
            load_down(own, turn).wait()
            term = jnp.dot(
                hidden_ref[own], down_ref[own, :, part], preferred_element_type=jnp.float32
            ) * weights[own]
            total = term if total is None else total + term
        total = total.astype(jnp.bfloat16)
        kept_ref[:, part] = total[:count]
        sent_ref[:, part] = total[count:]


def experts_of(own, got, first, experts, expert_gate, expert_up, expert_down):
    count, packed = own.shape
    owned, width, units = expert_gate.shape
    scalars = jnp.stack([first, jnp.int32(experts)])
    vmem = pl.BlockSpec(memory_space=pltpu.VMEM)
    hbm = pl.BlockSpec(memory_space=pltpu.HBM)
    half = jax.ShapeDtypeStruct((count, width), jnp.bfloat16)
    step = min(units, 256)
    wide = 512 if width % 512 == 0 else 128
    return pl.pallas_call(
        experts_kernel,
        out_shape=(half, half),
        in_specs=[pl.BlockSpec(memory_space=pltpu.SMEM), vmem, vmem, hbm, hbm, hbm],
        out_specs=(vmem, vmem),
        scratch_shapes=[
            pltpu.VMEM((2 * count, packed), jnp.bfloat16),
            pltpu.VMEM((owned, 2 * count, units), jnp.bfloat16),
            pltpu.VMEM(expert_gate.shape, jnp.bfloat16),
            pltpu.VMEM(expert_up.shape, jnp.bfloat16),
            pltpu.VMEM(expert_down.shape, jnp.bfloat16),
            pltpu.SemaphoreType.DMA((2, owned, units // step)),
            pltpu.SemaphoreType.DMA((owned, width // wide)),
        ],
        compiler_params=pltpu.CompilerParams(vmem_limit_bytes=VMEM_LIMIT),
        cost_estimate=pl.CostEstimate(
            flops=120 * count * owned * width * units,
            bytes_accessed=6 * owned * width * units,
            transcendentals=2 * count * owned * units,
        ),
        name="experts",
    )(scalars, own, got, expert_gate, expert_up, expert_down)


def attend(queries, new_latent, cache, lengths):
    steps = queries.shape[1]
    ctx = cache.shape[1]
    keys = jnp.concatenate([cache, new_latent], axis=1)
    scores = jnp.einsum("rshl,rkl->rshk", queries, keys, preferred_element_type=jnp.float32) * SCALE
    position = jnp.arange(ctx + steps)
    step_index = jnp.arange(steps)
    in_cache = position[None, :] < lengths[:, None]
    in_new = (position[None, :] >= ctx) & (position[None, :] - ctx <= step_index[:, None])
    allowed = in_cache[:, None, :] | in_new[None, :, :]
    scores = jnp.where(allowed[:, :, None, :], scores, -jnp.inf)
    top = jnp.max(scores, axis=-1, keepdims=True)
    weights = jnp.exp(scores - top)
    weights = (weights / jnp.sum(weights, axis=-1, keepdims=True)).astype(jnp.bfloat16)
    values = keys[:, :, :VDIM]
    return jnp.einsum("rshk,rkv->rshv", weights, values, preferred_element_type=jnp.float32).astype(
        jnp.bfloat16
    )


def body(
    prompt_pages,
    send_page,
    page_table,
    context_len,
    new_latent,
    queries,
    moe_rows,
    routing,
    gate_weights,
    expert_gate,
    expert_up,
    expert_down,
):
    peers = lax.axis_size("dev")
    pages = prompt_pages[0]
    outgoing_slots = send_page[0]
    page_len, width_lat = (pages.shape[1], pages.shape[2])
    capp = outgoing_slots.shape[0] // peers
    picked_pages = pages[jnp.maximum(outgoing_slots, 0)]
    arrived = lax.all_to_all(
        picked_pages.reshape(peers, capp, page_len, width_lat),
        "dev",
        split_axis=0,
        concat_axis=0,
        tiled=True,
    )
    arrived = arrived.reshape(peers * capp, page_len, width_lat)

    owned = expert_gate.shape[0]
    experts = peers * owned
    rows = routing.shape[1]
    width = moe_rows.shape[2]
    named = routing[0][:, :, None] == jnp.arange(experts)[None, None, :]
    dense = jnp.sum(jnp.where(named, gate_weights[0][:, :, None], 0.0), axis=1)
    high = dense.astype(jnp.bfloat16)
    low = (dense - high.astype(jnp.float32)).astype(jnp.bfloat16)
    extra = jnp.concatenate([high, low], axis=1)
    pad = -extra.shape[1] % 128
    packed = jnp.concatenate([moe_rows[0], jnp.pad(extra, ((0, 0), (0, pad)))], axis=1)
    far, near, last = levels_of(peers, lax.axis_size(("section", "tp")))
    pooled = packed[None]
    for bits in pairs_of(far):
        pooled = jnp.concatenate([pooled] + [exchange(pooled, mask) for mask in masks_of(bits)[1:]], axis=0)
    pooled = pooled.reshape(-1, packed.shape[1])
    pooled = jnp.concatenate([pooled] + [exchange(pooled, mask) for mask in masks_of(near)[1:]], axis=0)
    other = masks_of(last)[-1]
    first = lax.axis_index("dev") * owned
    kept, sent = experts_of(
        pooled, exchange(pooled, other), first, experts, expert_gate, expert_up, expert_down
    )
    mixed = kept.astype(jnp.float32) + exchange(sent, other).astype(jnp.float32)
    mixed = mixed.astype(jnp.bfloat16)
    masks = masks_of(near)
    mixed = mixed.reshape(len(masks), -1, width)
    got = [exchange(mixed[turn], masks[turn]) for turn in range(1, len(masks))]
    got[0], arrived = lax.optimization_barrier((got[0], arrived))
    total = mixed[0].astype(jnp.float32)
    for part in got:
        total = total + part.astype(jnp.float32)
    mixed = total.astype(jnp.bfloat16)
    for bits in pairs_of(far)[::-1]:
        mixed = collect(mixed, bits)

    table = page_table[0]
    requests, most_pages = table.shape
    cache = arrived[jnp.maximum(table, 0)].reshape(requests, most_pages * page_len, width_lat)
    attended = attend(queries[0], new_latent[0], cache, context_len[0])
    return (attended[None], mixed[None])


def solution(mesh):
    rank = ("grp",) + RANK
    return jax.shard_map(
        body,
        mesh=mesh,
        in_specs=(
            P(rank, None, None, None),
            P(rank, None),
            P(rank, None, None),
            P(rank, None),
            P(rank, None, None, None),
            P(rank, None, None, None, None),
            P(rank, None, None),
            P(rank, None, None),
            P(rank, None, None),
            P("dev", None, ("section", "tp")),
            P("dev", None, ("section", "tp")),
            P("dev", ("section", "tp"), None),
        ),
        out_specs=(
            P(rank, None, None, None, None),
            P(rank, None, None),
        ),
        check_vma=False,
    )
```

```python
import jax
import jax.numpy as jnp
from jax import lax
from jax.sharding import PartitionSpec as P

VDIM = 512
SCALE = 192.0 ** (-0.5)
RANK = ("dev", "section", "tp")


def gather_stages(peers, blocks):
    low = blocks.bit_length() - 1
    bits = peers.bit_length() - 1
    far = [low + bit for bit in range(2, bits)]
    near = list(range(low)) + [low + bit for bit in range(1, min(bits, 2))]
    last = [low + bit for bit in range(min(bits, 1))]
    stages = []
    for group in (far, near, last):
        stages += [group[at : at + 2] for at in range(0, len(group), 2)]
    return stages


def masks_of(stage):
    masks = [0]
    for bit in stage:
        masks += [mask | (1 << bit) for mask in masks]
    return masks


def exchange(value, mask):
    count = lax.axis_size(RANK)
    return lax.ppermute(value, RANK, [(at, at ^ mask) for at in range(count)])


def attend(queries, new_latent, cache, lengths):
    steps = queries.shape[1]
    ctx = cache.shape[1]
    keys = jnp.concatenate([cache, new_latent], axis=1)
    scores = jnp.einsum("rshl,rkl->rshk", queries, keys, preferred_element_type=jnp.float32) * SCALE
    position = jnp.arange(ctx + steps)
    step_index = jnp.arange(steps)
    in_cache = position[None, :] < lengths[:, None]
    in_new = (position[None, :] >= ctx) & (position[None, :] - ctx <= step_index[:, None])
    allowed = in_cache[:, None, :] | in_new[None, :, :]
    scores = jnp.where(allowed[:, :, None, :], scores, -jnp.inf)
    top = jnp.max(scores, axis=-1, keepdims=True)
    weights = jnp.exp(scores - top)
    weights = (weights / jnp.sum(weights, axis=-1, keepdims=True)).astype(jnp.bfloat16)
    values = keys[:, :, :VDIM]
    return jnp.einsum("rshk,rkv->rshv", weights, values, preferred_element_type=jnp.float32).astype(
        jnp.bfloat16
    )


def body(
    prompt_pages,
    send_page,
    page_table,
    context_len,
    new_latent,
    queries,
    moe_rows,
    routing,
    gate_weights,
    expert_gate,
    expert_up,
    expert_down,
):
    peers = lax.axis_size("dev")
    pages = prompt_pages[0]
    outgoing_slots = send_page[0]
    page_len, width_lat = (pages.shape[1], pages.shape[2])
    capp = outgoing_slots.shape[0] // peers
    picked_pages = pages[jnp.maximum(outgoing_slots, 0)]
    arrived = lax.all_to_all(
        picked_pages.reshape(peers, capp, page_len, width_lat),
        "dev",
        split_axis=0,
        concat_axis=0,
        tiled=True,
    )
    arrived = arrived.reshape(peers * capp, page_len, width_lat)

    owned = expert_gate.shape[0]
    experts = peers * owned
    rows = routing.shape[1]
    width = moe_rows.shape[2]
    named = routing[0][:, :, None] == jnp.arange(experts)[None, None, :]
    dense = jnp.sum(jnp.where(named, gate_weights[0][:, :, None], 0.0), axis=1)
    high = dense.astype(jnp.bfloat16)
    low = (dense - high.astype(jnp.float32)).astype(jnp.bfloat16)
    extra = jnp.concatenate([high, low], axis=1)
    pad = -extra.shape[1] % 128
    packed = jnp.concatenate([moe_rows[0], jnp.pad(extra, ((0, 0), (0, pad)))], axis=1)
    stages = gather_stages(peers, lax.axis_size(("section", "tp")))
    pooled = packed[None]
    for turn, stage in enumerate(stages):
        if turn == 1:
            pooled = pooled.reshape(-1, packed.shape[1])
        if turn == len(stages) - 1:
            pooled = lax.optimization_barrier(pooled)
        pooled = jnp.concatenate(
            [pooled] + [exchange(pooled, mask) for mask in masks_of(stage)[1:]], axis=0
        )
    every = pooled[:, :width]
    first = lax.axis_index("dev") * owned
    total = None
    for own in range(owned):
        column = width + first + own
        weight = lax.dynamic_slice_in_dim(pooled, column, 1, 1).astype(jnp.float32) + lax.dynamic_slice_in_dim(
            pooled, column + experts, 1, 1
        ).astype(jnp.float32)
        gate = jnp.dot(every, expert_gate[own], preferred_element_type=jnp.float32)
        up = jnp.dot(every, expert_up[own], preferred_element_type=jnp.float32)
        hidden = (jax.nn.silu(gate) * up).astype(jnp.bfloat16)
        term = jnp.dot(hidden, expert_down[own], preferred_element_type=jnp.float32) * weight
        total = term if total is None else total + term
    mixed = total.astype(jnp.bfloat16)
    for stage in stages[::-1]:
        masks = masks_of(stage)
        count = mixed.shape[0] // len(masks)
        kept = mixed[:count].astype(jnp.float32)
        for turn in range(1, len(masks)):
            sent = mixed[turn * count : (turn + 1) * count]
            kept = kept + exchange(sent, masks[turn]).astype(jnp.float32)
        mixed = kept.astype(jnp.bfloat16)

    table = page_table[0]
    requests, most_pages = table.shape
    cache = arrived[jnp.maximum(table, 0)].reshape(requests, most_pages * page_len, width_lat)
    attended = attend(queries[0], new_latent[0], cache, context_len[0])
    return (attended[None], mixed[None])


def solution(mesh):
    rank = ("grp",) + RANK
    return jax.shard_map(
        body,
        mesh=mesh,
        in_specs=(
            P(rank, None, None, None),
            P(rank, None),
            P(rank, None, None),
            P(rank, None),
            P(rank, None, None, None),
            P(rank, None, None, None, None),
            P(rank, None, None),
            P(rank, None, None),
            P(rank, None, None),
            P("dev", None, ("section", "tp")),
            P("dev", None, ("section", "tp")),
            P("dev", ("section", "tp"), None),
        ),
        out_specs=(
            P(rank, None, None, None, None),
            P(rank, None, None),
        ),
        check_vma=False,
    )
```

```python
import functools

import jax
import jax.numpy as jnp
from jax import lax
from jax.experimental import pallas as pl
from jax.experimental.pallas import tpu as pltpu
from jax.sharding import PartitionSpec as P

VDIM = 512
SCALE = 192.0 ** (-0.5)
RANK = ("dev", "section", "tp")


def gather_stages(peers, blocks):
    low = blocks.bit_length() - 1
    bits = peers.bit_length() - 1
    far = [low + bit for bit in range(2, bits)]
    near = list(range(low)) + [low + bit for bit in range(1, min(bits, 2))]
    last = [low + bit for bit in range(min(bits, 1))]
    stages = []
    for group in (far, near, last):
        stages += [group[at : at + 2] for at in range(0, len(group), 2)]
    return stages


def masks_of(stage):
    masks = [0]
    for bit in stage:
        masks += [mask | (1 << bit) for mask in masks]
    return masks


def exchange(value, mask):
    count = lax.axis_size(RANK)
    return lax.ppermute(value, RANK, [(at, at ^ mask) for at in range(count)])


def pack_kernel(experts, rows_ref, routing_ref, weights_ref, out_ref):
    rows, width = rows_ref.shape
    lanes = out_ref.shape[1] - width
    out_ref[:, :width] = rows_ref[...]
    lane = lax.broadcasted_iota(jnp.int32, (rows, lanes), 1)
    expert = jnp.where(lane < experts, lane, lane - experts)
    dense = jnp.zeros((rows, lanes), jnp.float32)
    for turn in range(routing_ref.shape[1]):
        named = routing_ref[:, turn : turn + 1] == expert
        dense = dense + jnp.where(named, weights_ref[:, turn : turn + 1], 0.0)
    high = dense.astype(jnp.bfloat16).astype(jnp.float32)
    out_ref[:, width:] = jnp.where(lane < experts, high, dense - high).astype(jnp.bfloat16)


def pack(rows, routing, weights, experts):
    lanes = -(-2 * experts // 128) * 128
    vmem = pl.BlockSpec(memory_space=pltpu.VMEM)
    return pl.pallas_call(
        functools.partial(pack_kernel, experts),
        out_shape=jax.ShapeDtypeStruct((rows.shape[0], rows.shape[1] + lanes), rows.dtype),
        in_specs=[vmem, vmem, vmem],
        out_specs=vmem,
        name="pack",
    )(rows, routing, weights)


def attend(queries, new_latent, cache, lengths):
    steps = queries.shape[1]
    ctx = cache.shape[1]
    keys = jnp.concatenate([cache, new_latent], axis=1)
    scores = jnp.einsum("rshl,rkl->rshk", queries, keys, preferred_element_type=jnp.float32) * SCALE
    position = jnp.arange(ctx + steps)
    step_index = jnp.arange(steps)
    in_cache = position[None, :] < lengths[:, None]
    in_new = (position[None, :] >= ctx) & (position[None, :] - ctx <= step_index[:, None])
    allowed = in_cache[:, None, :] | in_new[None, :, :]
    scores = jnp.where(allowed[:, :, None, :], scores, -jnp.inf)
    top = jnp.max(scores, axis=-1, keepdims=True)
    weights = jnp.exp(scores - top)
    weights = (weights / jnp.sum(weights, axis=-1, keepdims=True)).astype(jnp.bfloat16)
    values = keys[:, :, :VDIM]
    return jnp.einsum("rshk,rkv->rshv", weights, values, preferred_element_type=jnp.float32).astype(
        jnp.bfloat16
    )


def body(
    prompt_pages,
    send_page,
    page_table,
    context_len,
    new_latent,
    queries,
    moe_rows,
    routing,
    gate_weights,
    expert_gate,
    expert_up,
    expert_down,
):
    peers = lax.axis_size("dev")
    pages = prompt_pages[0]
    outgoing_slots = send_page[0]
    page_len, width_lat = (pages.shape[1], pages.shape[2])
    capp = outgoing_slots.shape[0] // peers
    picked_pages = pages[jnp.maximum(outgoing_slots, 0)]
    arrived = lax.all_to_all(
        picked_pages.reshape(peers, capp, page_len, width_lat),
        "dev",
        split_axis=0,
        concat_axis=0,
        tiled=True,
    )
    arrived = arrived.reshape(peers * capp, page_len, width_lat)

    owned = expert_gate.shape[0]
    experts = peers * owned
    rows = routing.shape[1]
    width = moe_rows.shape[2]
    packed = pack(moe_rows[0], routing[0], gate_weights[0], experts)
    stages = gather_stages(peers, lax.axis_size(("section", "tp")))
    pooled = packed[None]
    for turn, stage in enumerate(stages):
        if turn == 1:
            pooled = pooled.reshape(-1, packed.shape[1])
        if turn == len(stages) - 1:
            pooled = lax.optimization_barrier(pooled)
        pooled = jnp.concatenate(
            [pooled] + [exchange(pooled, mask) for mask in masks_of(stage)[1:]], axis=0
        )
    every = pooled[:, :width]
    first = lax.axis_index("dev") * owned
    total = None
    for own in range(owned):
        column = width + first + own
        weight = lax.dynamic_slice_in_dim(pooled, column, 1, 1).astype(jnp.float32) + lax.dynamic_slice_in_dim(
            pooled, column + experts, 1, 1
        ).astype(jnp.float32)
        gate = jnp.dot(every, expert_gate[own], preferred_element_type=jnp.float32)
        up = jnp.dot(every, expert_up[own], preferred_element_type=jnp.float32)
        hidden = (jax.nn.silu(gate) * up).astype(jnp.bfloat16)
        term = jnp.dot(hidden, expert_down[own], preferred_element_type=jnp.float32) * weight
        total = term if total is None else total + term
    mixed = total.astype(jnp.bfloat16)
    for stage in stages[::-1]:
        masks = masks_of(stage)
        count = mixed.shape[0] // len(masks)
        kept = mixed[:count].astype(jnp.float32)
        for turn in range(1, len(masks)):
            sent = mixed[turn * count : (turn + 1) * count]
            kept = kept + exchange(sent, masks[turn]).astype(jnp.float32)
        mixed = kept.astype(jnp.bfloat16)

    table = page_table[0]
    requests, most_pages = table.shape
    cache = arrived[jnp.maximum(table, 0)].reshape(requests, most_pages * page_len, width_lat)
    attended = attend(queries[0], new_latent[0], cache, context_len[0])
    return (attended[None], mixed[None])


def solution(mesh):
    rank = ("grp",) + RANK
    return jax.shard_map(
        body,
        mesh=mesh,
        in_specs=(
            P(rank, None, None, None),
            P(rank, None),
            P(rank, None, None),
            P(rank, None),
            P(rank, None, None, None),
            P(rank, None, None, None, None),
            P(rank, None, None),
            P(rank, None, None),
            P(rank, None, None),
            P("dev", None, ("section", "tp")),
            P("dev", None, ("section", "tp")),
            P("dev", ("section", "tp"), None),
        ),
        out_specs=(
            P(rank, None, None, None, None),
            P(rank, None, None),
        ),
        check_vma=False,
    )
```

```python
import jax
import jax.numpy as jnp
from jax import lax
from jax.sharding import PartitionSpec as P

VDIM = 512
SCALE = 192.0 ** (-0.5)
RANK = ("dev", "section", "tp")


def gather_stages(peers, blocks):
    low = blocks.bit_length() - 1
    bits = peers.bit_length() - 1
    far = [low + bit for bit in range(2, bits)]
    near = list(range(low)) + [low + bit for bit in range(1, min(bits, 2))]
    last = [low + bit for bit in range(min(bits, 1))]
    stages = []
    for group in (far, near, last):
        stages += [group[at : at + 2] for at in range(0, len(group), 2)]
    return stages


def masks_of(stage):
    masks = [0]
    for bit in stage:
        masks += [mask | (1 << bit) for mask in masks]
    return masks


def exchange(value, mask):
    count = lax.axis_size(RANK)
    return lax.ppermute(value, RANK, [(at, at ^ mask) for at in range(count)])


def attend(queries, new_latent, cache, lengths):
    steps = queries.shape[1]
    ctx = cache.shape[1]
    keys = jnp.concatenate([cache, new_latent], axis=1)
    scores = jnp.einsum("rshl,rkl->rshk", queries, keys, preferred_element_type=jnp.float32) * SCALE
    position = jnp.arange(ctx + steps)
    step_index = jnp.arange(steps)
    in_cache = position[None, :] < lengths[:, None]
    in_new = (position[None, :] >= ctx) & (position[None, :] - ctx <= step_index[:, None])
    allowed = in_cache[:, None, :] | in_new[None, :, :]
    scores = jnp.where(allowed[:, :, None, :], scores, -jnp.inf)
    top = jnp.max(scores, axis=-1, keepdims=True)
    scores, top = lax.optimization_barrier((scores, top))
    weights = jnp.exp(scores - top)
    weights = (weights / jnp.sum(weights, axis=-1, keepdims=True)).astype(jnp.bfloat16)
    values = keys[:, :, :VDIM]
    return jnp.einsum("rshk,rkv->rshv", weights, values, preferred_element_type=jnp.float32).astype(
        jnp.bfloat16
    )


def body(
    prompt_pages,
    send_page,
    page_table,
    context_len,
    new_latent,
    queries,
    moe_rows,
    routing,
    gate_weights,
    expert_gate,
    expert_up,
    expert_down,
):
    peers = lax.axis_size("dev")
    pages = prompt_pages[0]
    outgoing_slots = send_page[0]
    page_len, width_lat = (pages.shape[1], pages.shape[2])
    capp = outgoing_slots.shape[0] // peers
    picked_pages = pages[jnp.maximum(outgoing_slots, 0)]
    arrived = lax.all_to_all(
        picked_pages.reshape(peers, capp, page_len, width_lat),
        "dev",
        split_axis=0,
        concat_axis=0,
        tiled=True,
    )
    arrived = arrived.reshape(peers * capp, page_len, width_lat)

    owned = expert_gate.shape[0]
    experts = peers * owned
    rows = routing.shape[1]
    width = moe_rows.shape[2]
    named = routing[0][:, :, None] == jnp.arange(experts)[None, None, :]
    dense = jnp.sum(jnp.where(named, gate_weights[0][:, :, None], 0.0), axis=1)
    high = dense.astype(jnp.bfloat16)
    low = (dense - high.astype(jnp.float32)).astype(jnp.bfloat16)
    extra = jnp.concatenate([high, low], axis=1)
    pad = -extra.shape[1] % 128
    packed = jnp.concatenate([moe_rows[0], jnp.pad(extra, ((0, 0), (0, pad)))], axis=1)
    stages = gather_stages(peers, lax.axis_size(("section", "tp")))
    pooled = packed[None]
    for turn, stage in enumerate(stages):
        if turn == 1:
            pooled = pooled.reshape(-1, packed.shape[1])
        if turn == len(stages) - 1:
            pooled = lax.optimization_barrier(pooled)
        pooled = jnp.concatenate(
            [pooled] + [exchange(pooled, mask) for mask in masks_of(stage)[1:]], axis=0
        )
    every = pooled[:, :width]
    first = lax.axis_index("dev") * owned
    total = None
    for own in range(owned):
        column = width + first + own
        weight = lax.dynamic_slice_in_dim(pooled, column, 1, 1).astype(jnp.float32) + lax.dynamic_slice_in_dim(
            pooled, column + experts, 1, 1
        ).astype(jnp.float32)
        gate = jnp.dot(every, expert_gate[own], preferred_element_type=jnp.float32)
        up = jnp.dot(every, expert_up[own], preferred_element_type=jnp.float32)
        hidden = (jax.nn.silu(gate) * up).astype(jnp.bfloat16)
        term = jnp.dot(hidden, expert_down[own], preferred_element_type=jnp.float32) * weight
        total = term if total is None else total + term
    mixed = total.astype(jnp.bfloat16)
    for stage in stages[::-1]:
        masks = masks_of(stage)
        count = mixed.shape[0] // len(masks)
        kept = mixed[:count].astype(jnp.float32)
        for turn in range(1, len(masks)):
            sent = mixed[turn * count : (turn + 1) * count]
            kept = kept + exchange(sent, masks[turn]).astype(jnp.float32)
        mixed = kept.astype(jnp.bfloat16)

    table = page_table[0]
    requests, most_pages = table.shape
    cache = arrived[jnp.maximum(table, 0)].reshape(requests, most_pages * page_len, width_lat)
    attended = attend(queries[0], new_latent[0], cache, context_len[0])
    return (attended[None], mixed[None])


def solution(mesh):
    rank = ("grp",) + RANK
    return jax.shard_map(
        body,
        mesh=mesh,
        in_specs=(
            P(rank, None, None, None),
            P(rank, None),
            P(rank, None, None),
            P(rank, None),
            P(rank, None, None, None),
            P(rank, None, None, None, None),
            P(rank, None, None),
            P(rank, None, None),
            P(rank, None, None),
            P("dev", None, ("section", "tp")),
            P("dev", None, ("section", "tp")),
            P("dev", ("section", "tp"), None),
        ),
        out_specs=(
            P(rank, None, None, None, None),
            P(rank, None, None),
        ),
        check_vma=False,
    )
```

```python
import jax
import jax.numpy as jnp
from jax import lax
from jax.sharding import PartitionSpec as P

VDIM = 512
SCALE = 192.0 ** (-0.5)
RANK = ("dev", "section", "tp")


def gather_stages(peers, blocks):
    low = blocks.bit_length() - 1
    bits = peers.bit_length() - 1
    far = [low + bit for bit in range(2, bits)]
    near = list(range(low)) + [low + bit for bit in range(1, min(bits, 2))]
    last = [low + bit for bit in range(min(bits, 1))]
    stages = []
    for group in (far, near, last):
        stages += [group[at : at + 2] for at in range(0, len(group), 2)]
    return stages


def masks_of(stage):
    masks = [0]
    for bit in stage:
        masks += [mask | (1 << bit) for mask in masks]
    return masks


def exchange(value, mask):
    count = lax.axis_size(RANK)
    return lax.ppermute(value, RANK, [(at, at ^ mask) for at in range(count)])


def attend(queries, new_latent, cache, lengths):
    steps = queries.shape[1]
    ctx = cache.shape[1]
    keys = jnp.concatenate([cache, new_latent], axis=1)
    scores = jnp.einsum("rshl,rkl->rshk", queries, keys, preferred_element_type=jnp.float32) * SCALE
    position = jnp.arange(ctx + steps)
    step_index = jnp.arange(steps)
    in_cache = position[None, :] < lengths[:, None]
    in_new = (position[None, :] >= ctx) & (position[None, :] - ctx <= step_index[:, None])
    allowed = in_cache[:, None, :] | in_new[None, :, :]
    scores = jnp.where(allowed[:, :, None, :], scores, -jnp.inf)
    top = jnp.max(scores, axis=-1, keepdims=True)
    scores, top = lax.optimization_barrier((scores, top))
    weights = jnp.exp(scores - top)
    weights = (weights / jnp.sum(weights, axis=-1, keepdims=True)).astype(jnp.bfloat16)
    values = keys[:, :, :VDIM]
    return jnp.einsum("rshk,rkv->rshv", weights, values, preferred_element_type=jnp.float32).astype(
        jnp.bfloat16
    )


def body(
    prompt_pages,
    send_page,
    page_table,
    context_len,
    new_latent,
    queries,
    moe_rows,
    routing,
    gate_weights,
    expert_gate,
    expert_up,
    expert_down,
):
    peers = lax.axis_size("dev")
    pages = prompt_pages[0]
    outgoing_slots = send_page[0]
    page_len, width_lat = (pages.shape[1], pages.shape[2])
    capp = outgoing_slots.shape[0] // peers
    picked_pages = pages.at[outgoing_slots].get(mode="clip", wrap_negative_indices=False)
    arrived = lax.all_to_all(
        picked_pages.reshape(peers, capp, page_len, width_lat),
        "dev",
        split_axis=0,
        concat_axis=0,
        tiled=True,
    )
    arrived = arrived.reshape(peers * capp, page_len, width_lat)

    owned = expert_gate.shape[0]
    experts = peers * owned
    rows = routing.shape[1]
    width = moe_rows.shape[2]
    named = routing[0][:, :, None] == jnp.arange(experts)[None, None, :]
    dense = jnp.sum(jnp.where(named, gate_weights[0][:, :, None], 0.0), axis=1)
    high = dense.astype(jnp.bfloat16)
    low = (dense - high.astype(jnp.float32)).astype(jnp.bfloat16)
    extra = jnp.concatenate([high, low], axis=1)
    pad = -extra.shape[1] % 128
    packed = jnp.concatenate([moe_rows[0], jnp.pad(extra, ((0, 0), (0, pad)))], axis=1)
    stages = gather_stages(peers, lax.axis_size(("section", "tp")))
    pooled = packed[None]
    for turn, stage in enumerate(stages):
        if turn == 1:
            pooled = pooled.reshape(-1, packed.shape[1])
        if turn == len(stages) - 1:
            pooled = lax.optimization_barrier(pooled)
        pooled = jnp.concatenate(
            [pooled] + [exchange(pooled, mask) for mask in masks_of(stage)[1:]], axis=0
        )
    every = pooled[:, :width]
    first = lax.axis_index("dev") * owned
    total = None
    for own in range(owned):
        column = width + first + own
        weight = lax.dynamic_slice_in_dim(pooled, column, 1, 1).astype(jnp.float32) + lax.dynamic_slice_in_dim(
            pooled, column + experts, 1, 1
        ).astype(jnp.float32)
        gate = jnp.dot(every, expert_gate[own], preferred_element_type=jnp.float32)
        up = jnp.dot(every, expert_up[own], preferred_element_type=jnp.float32)
        hidden = (jax.nn.silu(gate) * up).astype(jnp.bfloat16)
        term = jnp.dot(hidden, expert_down[own], preferred_element_type=jnp.float32) * weight
        total = term if total is None else total + term
    mixed = total.astype(jnp.bfloat16)
    for stage in stages[::-1]:
        masks = masks_of(stage)
        count = mixed.shape[0] // len(masks)
        kept = mixed[:count].astype(jnp.float32)
        for turn in range(1, len(masks)):
            sent = mixed[turn * count : (turn + 1) * count]
            kept = kept + exchange(sent, masks[turn]).astype(jnp.float32)
        mixed = kept.astype(jnp.bfloat16)

    table = page_table[0]
    requests, most_pages = table.shape
    cache = arrived.at[table].get(mode="clip", wrap_negative_indices=False).reshape(requests, most_pages * page_len, width_lat)
    attended = attend(queries[0], new_latent[0], cache, context_len[0])
    return (attended[None], mixed[None])


def solution(mesh):
    rank = ("grp",) + RANK
    return jax.shard_map(
        body,
        mesh=mesh,
        in_specs=(
            P(rank, None, None, None),
            P(rank, None),
            P(rank, None, None),
            P(rank, None),
            P(rank, None, None, None),
            P(rank, None, None, None, None),
            P(rank, None, None),
            P(rank, None, None),
            P(rank, None, None),
            P("dev", None, ("section", "tp")),
            P("dev", None, ("section", "tp")),
            P("dev", ("section", "tp"), None),
        ),
        out_specs=(
            P(rank, None, None, None, None),
            P(rank, None, None),
        ),
        check_vma=False,
    )
```
